512 devices in a mesh: dom: 64 (over x, y, z_lo), band: 8 (over z_hi, core).
Axes of the slice: x: 4, y: 8, z: 8 (z_hi: 4, z_lo: 2; z = z_hi * 2 + z_lo), core: 2. Of those that a mesh axis runs over, the one named last changes fastest.
Arguments:
- orbitals: float32 [128, 512, 648], P('band', 'dom'), may hold values from -6 to 6
- cell_operator: float32 [729, 729], replicated, may hold values from -0.21875 to 0.21875
- cell_scale: float32 [512], P('dom'), may hold values from 0.5 to 2
- density: float32 [131072, 729], P(('dom', 'band')), may hold values from 0.01 to 1
- block_owner: int32 [131072, 1], P(('dom', 'band')), may hold values from 0 to 63; in each aligned block of 256 rows (0 to 255, 256 to 511, ...) at most 8 rows name the same one
- block_cell: int32 [131072], P(('dom', 'band')), may hold values from 0 to 7
Outputs:
- basis: float32 [128, 512, 648], P(None, ('dom', 'band'))
The draws below stay inside these ranges and needn't reach their ends.
Inputs may be any that keep to these rules, and one draw needn't show every extreme that they name: `block_owner`: among the rows of one device no domain is named more than 8 times, a bound that some block reaches.
All inputs are finite; a program needn't handle non-finite values.
Results may differ from the reference program's by a relative error of at most 0.000071.
Values sent between devices are 32-bit elements; how exact they have to be, the bound alone decides.
No kernel may reach another device: no remote copies, remote signals or barrier semaphores. Data moves between devices by JAX's collectives and lax.ppermute only.
A program may use at most 64 MiB of HBM per device.

```python
import math
import jax
import jax.numpy as jnp
import numpy as np
from jax import lax

CELLS_DOM = 8
NB = 128
CAP = 8
CELL_NODES = 729
FACE = 81
OWN = 648
CELLS = 512
RB = 256
BLOCKS = 131072
N_DOM = 64


def touch_ends(values, stream_key, low, top_value):
    dims = values.shape
    spot = [jax.random.randint(jax.random.fold_in(stream_key, axis), (), 0, dims[axis]) for axis in range(len(dims))]
    values = values.at[tuple(spot)].set(low)
    longest = dims.index(max(dims))
    spot[longest] = (spot[longest] + 1) % dims[longest]
    return values.at[tuple(spot)].set(top_value)


def shard_levels(stream_key, dims, pieces, low, top_value):
    loudness = 1.0
    for position, parts in pieces:
        heights = jax.random.uniform(jax.random.fold_in(jax.random.fold_in(stream_key, 6), position), (parts,), jnp.float32, low / len(pieces), top_value / len(pieces))
        loudness = loudness * jnp.repeat(jnp.exp(heights), dims[position] // parts).reshape((-1,) + (1,) * (len(dims) - 1 - position))
    return loudness


def routed_block(key, own, number, rows, count, top, reach, skew):
    ranking = jax.random.permutation(key, count)
    crowded, common = portions_of(count, rows * top, reach, skew, True), portions_of(count, rows * top, reach, skew, False)
    places = jnp.arange(count)

    def named(sizes, rotation):
        used = int((sizes > 0).sum())
        fixed = max(1, used // 4)
        moved = fixed + (places - fixed + rotation * (used - fixed)) % max(1, count - fixed)
        return jnp.zeros((count,), jnp.int32).at[ranking[jnp.where(places < fixed, places, moved)]].set(jnp.asarray(sizes, jnp.int32))

    sizes = jnp.where(number % 4 == 0, named(crowded, number // 4), named(common, number - number // 4 - 1))
    mixed = jax.random.permutation(jax.random.fold_in(own, 3), count)
    donor, sink = mixed[0:count // 2 * 2:2], mixed[1:count // 2 * 2:2]
    room = jnp.minimum(sizes[donor] - 1, reach - sizes[sink]) // 2
    room = jnp.where((donor == ranking[0]) | (sink == ranking[0]) | (sizes[sink] == 0), 0, jnp.maximum(room, 0))
    moved = jax.random.randint(jax.random.fold_in(own, 4), (count // 2,), 0, 1 << 20) % (room + 1)
    sizes = sizes.at[donor].add(-moved).at[sink].add(moved)
    items = jnp.searchsorted(jnp.cumsum(sizes), jnp.arange(rows * top), side="right").astype(jnp.int32)
    table = items.reshape(top, rows).T
    table = table[jax.random.permutation(jax.random.fold_in(own, 1), rows)]
    rotation = jax.random.randint(jax.random.fold_in(own, 2), (rows, 1), 0, top)
    return jnp.take_along_axis(table, (jnp.arange(top)[None, :] + rotation) % top, axis=1)


def portions_of(amount, total, bound, skew, full):
    portions = [(1 << 20) // math.isqrt(grade ** skew) + 1 for grade in range(1, amount + 1)]
    largest = bound if full else min(bound, max(-(-total // amount), total * portions[0] // sum(portions)))
    least = 1 if total - largest >= amount - 1 else 0
    holding, spare = [largest] + [least] * (amount - 1), total - largest - least * (amount - 1)
    while spare > 0:
        candidates = [i for i in range(1, amount) if holding[i] < largest] or [i for i in range(1, amount) if holding[i] < bound]
        pool, budget = sum([portions[i] for i in candidates]), spare
        for i in candidates:
            extra = min(bound - holding[i], max(1, budget * portions[i] // pool), spare)
            holding[i] = holding[i] + extra
            spare = spare - extra
    return np.array(holding)


def centred(own_key, dims, width, reach, shards=(), kind=jnp.bfloat16):
    array = jax.random.normal(own_key, dims, jnp.float32) * width
    if len(shards) > 0:
        array = shard_levels(own_key, dims, shards, -0.22, 0.18) * array
    return jnp.clip(array, min=-reach, max=reach).astype(kind)


def setup_inputs(seed: int = 0) -> dict:
    streams_of = jax.random.split(jax.random.key(seed), 7)
    orbitals = centred(streams_of[0], (NB, CELLS, OWN), 1.0, 6.0, ((0, 8), (1, 64)), jnp.float32)
    cell_operator = centred(streams_of[1], (CELL_NODES, CELL_NODES), CELL_NODES ** -0.5, 0.21875, (), jnp.float32)
    cell_scale = jnp.clip(jnp.exp(math.log(2.0) - 1.3862944 * jax.random.uniform(streams_of[2], (CELLS,), jnp.float32) ** shard_levels(streams_of[2], (CELLS,), ((0, 64),), -0.2, 0.2)), 0.5, 2.0)
    density = jnp.clip(jnp.exp(math.log(1.0) - 4.6051702 * jax.random.uniform(streams_of[3], (BLOCKS, CELL_NODES), jnp.float32) ** shard_levels(streams_of[3], (BLOCKS, CELL_NODES), ((0, 512),), -0.2, 0.2)), 0.01, 1.0)
    block_owner_keys = jax.random.split(jax.random.fold_in(streams_of[4], 1), BLOCKS // RB)
    block_owner_turns = jax.random.permutation(jax.random.fold_in(streams_of[4], 3), BLOCKS // RB)
    block_owner = jax.vmap(lambda own, number: routed_block(jax.random.fold_in(streams_of[4], 2), own, number, RB, N_DOM, 1, CAP, 2))(block_owner_keys, block_owner_turns).reshape((BLOCKS, 1))
    block_cell = touch_ends(jax.random.randint(streams_of[5], (BLOCKS,), 0, CELLS_DOM), jax.random.fold_in(streams_of[5], 1), 0, CELLS_DOM - 1).astype(jnp.int32)
    return dict(orbitals=orbitals, cell_operator=cell_operator, cell_scale=cell_scale, density=density, block_owner=block_owner, block_cell=block_cell)


CENTER = -1.0
HALF_WIDTH = 2.5

def apply_operator(field, scales, potential, operator):
    count = field.shape[0]
    zeros = jnp.zeros((count, 1, FACE), jnp.float32)
    layer = jnp.concatenate([field[:, 1:, :FACE], zeros], 1)
    cellvec = jnp.concatenate([field, layer], 2)
    product = jnp.einsum('ncj,jk->nck', cellvec, operator, precision=lax.Precision.HIGHEST)
    result = scales[None, :, None] * product + potential[None] * cellvec
    owned = result[:, :, :OWN]
    tail = result[:, :, OWN:]
    addition = jnp.concatenate([zeros, tail[:, :-1]], 1)
    return jnp.concatenate([owned[:, :, :FACE] + addition, owned[:, :, FACE:]], 2)

def reference(orbitals, cell_operator, cell_scale, density, block_owner, block_cell):
    target = (block_owner[:, 0] * CELLS_DOM + block_cell).astype(jnp.int32)
    rho = jax.ops.segment_sum(density, target, num_segments=CELLS)
    potential = -0.7386 * jnp.cbrt(rho)

    def step(field):
        return (apply_operator(field, cell_scale, potential, cell_operator) - CENTER * field) / HALF_WIDTH
    first = step(orbitals)
    second = 2.0 * step(first) - orbitals
    filtered = 2.0 * step(second) - first
    flat = filtered.reshape(NB, -1)
    intersection = jnp.dot(flat, flat.T, precision=lax.Precision.HIGHEST) / flat.shape[1]
    lower = jnp.linalg.cholesky(intersection)
    basis = jax.scipy.linalg.solve_triangular(lower, flat, lower=True)
    return basis.reshape(NB, CELLS, OWN)
```

```python
import jax
import jax.numpy as jnp
from jax import lax
from jax.experimental import pallas as pl
from jax.experimental.pallas import tpu as pltpu
from jax.sharding import PartitionSpec as P

FACE = 81
OWN = 648
NODES = 729
WIDE = 768
HALF = 384
SLAB = 136
TILE5 = 640
SPLIT = OWN - TILE5

CENTER = -1.0
HALF_WIDTH = 2.5

X_GROUPS = [[x * 16 + r for x in range(4)] for r in range(16)]
YZ_GROUPS = [[x * 16 + r for r in range(16)] for x in range(4)]


def exchange(value, axis, groups=None):
    return lax.all_to_all(value, axis, split_axis=0, concat_axis=0, tiled=True, axis_index_groups=groups)


def split2(value):
    high = value.astype(jnp.bfloat16)
    low = (value - high.astype(jnp.float32)).astype(jnp.bfloat16)
    return high, low


def dot(a, b):
    return jnp.dot(a, b, preferred_element_type=jnp.float32)


def deliver_kernel(core_ref, target_ref, density_ref, mine_ref, theirs_ref, wide_ref):
    rows = 4 * SLAB
    count = density_ref.shape[0]
    wide_ref[:, TILE5:] = jnp.zeros((count, WIDE - TILE5), jnp.float32)
    wide_ref[:, :NODES] = density_ref[...]
    row = lax.broadcasted_iota(jnp.int32, (rows, count), 0)
    slab = (row >= SLAB).astype(jnp.int32) + (row >= 2 * SLAB).astype(jnp.int32) + (row >= 3 * SLAB).astype(jnp.int32)
    cell = row - 8 * slab - 3
    onehot = jnp.where(target_ref[...] == cell, 1.0, 0.0).astype(jnp.bfloat16)
    for half in range(2):
        values = wide_ref[:, half * HALF:(half + 1) * HALF]
        first = values.astype(jnp.bfloat16)
        rest = values - first.astype(jnp.float32)
        second = rest.astype(jnp.bfloat16)
        third = (rest - second.astype(jnp.float32)).astype(jnp.bfloat16)
        total = dot(onehot, first) + dot(onehot, second) + dot(onehot, third)

        @pl.when(core_ref[0] == half)
        def _():
            mine_ref[...] = total

        @pl.when(core_ref[0] != half)
        def _():
            theirs_ref[...] = total


def filter_kernel(last_ref, own_ref, left_ref, right_ref, scale_ref, rho_ref, operator_ref, out_ref,
                  kwide, khigh, klow, v0, v1, v2, chigh, clow, cell_buf, product, pot):
    kwide[720:, :] = jnp.zeros((WIDE - 720, WIDE), jnp.float32)
    kwide[:, TILE5:] = jnp.zeros((WIDE, WIDE - TILE5), jnp.float32)
    kwide[:NODES, :NODES] = operator_ref[...]
    for i in range(0, WIDE, 128):
        high, low = split2(kwide[i:i + 128, :])
        khigh[i:i + 128, :] = high
        klow[i:i + 128, :] = low
    for half in range(2):
        rho = rho_ref[half]
        pot[:, half * HALF:(half + 1) * HALF] = jnp.where(
            rho > 0.0, -0.7386 * jnp.exp(jnp.log(jnp.where(rho > 0.0, rho, 1.0)) * (1.0 / 3.0)), 0.0)
    lane = lax.broadcasted_iota(jnp.int32, (16, 128), 1)
    is_face = lane < FACE
    is_own5 = lane < SPLIT
    zero5 = jnp.zeros((16, WIDE - TILE5), jnp.float32)

    def place(i, value):
        v0[16 * i:16 * i + 16, TILE5:] = zero5
        v0[16 * i:16 * i + 16, :OWN] = value

    for i in range(3):
        place(i, left_ref[i])
        place(11 + i, right_ref[i])
    for i in range(8):
        place(3 + i, own_ref[i])

    def scale_of(i):
        if i < 3:
            line = left_ref[3, 5 + i:6 + i, :128]
        elif i < 11:
            line = scale_ref[i - 3:i - 2, :]
        else:
            line = right_ref[3, i - 11:i - 10, :128]
        return line

    alive = last_ref[0].astype(jnp.float32)

    def apply(source, begin, end, combine):
        for i in range(begin, end):
            r = slice(16 * i, 16 * i + 16)
            n = slice(16 * i + 16, 16 * i + 32)
            for t in range(6):
                c = slice(128 * t, 128 * t + 128)
                value = source[r, c]
                if t == 5:
                    face = jnp.where(is_face, source[n, :128], 0.0)
                    value = value + pltpu.roll(face, SPLIT, 1)
                cell_buf[r, c] = value
                high, low = split2(value)
                chigh[r, c] = high
                clow[r, c] = low
        r = slice(16 * begin, 16 * end)
        a, b = chigh[r, :], clow[r, :]
        product[r, :] = dot(a, khigh[...]) + dot(b, khigh[...]) + dot(a, klow[...])
        tail = None
        for i in range(begin, end):
            r = slice(16 * i, 16 * i + 16)
            scale = scale_of(i)
            parts = []
            for t in range(6):
                c = slice(128 * t, 128 * t + 128)
                parts.append(scale * product[r, c] + pot[i:i + 1, c] * cell_buf[r, c])
            if tail is not None:
                add = jnp.where(is_face, pltpu.roll(tail, 128 - SPLIT, 1), 0.0)
                if i == 11:
                    add = add * alive
                parts[0] = parts[0] + add
                for t in range(6):
                    value = parts[t]
                    if t == 5:
                        value = jnp.where(is_own5, value, 0.0)
                    combine(i, t, value)
            tail = parts[5]

    def at(ref, i, t):
        return ref[16 * i:16 * i + 16, 128 * t:128 * t + 128]

    def first(i, t, value):
        v1[16 * i:16 * i + 16, 128 * t:128 * t + 128] = (value - CENTER * at(v0, i, t)) * (1.0 / HALF_WIDTH)

    def second(i, t, value):
        v2[16 * i:16 * i + 16, 128 * t:128 * t + 128] = (value - CENTER * at(v1, i, t)) * (2.0 / HALF_WIDTH) - at(v0, i, t)

    def third(i, t, value):
        result = (value - CENTER * at(v2, i, t)) * (2.0 / HALF_WIDTH) - at(v1, i, t)
        if t < 5:
            out_ref[i - 3, :, 128 * t:128 * t + 128] = result
        else:
            out_ref[i - 3, :, TILE5:OWN] = result[:, :SPLIT]

    apply(v0, 0, 13, first)
    apply(v1, 1, 12, second)
    apply(v2, 2, 11, third)


def body(orbitals, cell_operator, cell_scale, density, block_owner, block_cell):
    dom_count = lax.axis_size("dom")
    band_count = lax.axis_size("band")
    dom = lax.axis_index("dom")
    core = jnp.reshape(lax.axis_index("band") % 2, (1,)).astype(jnp.int32)
    alive = jnp.reshape((dom < dom_count - 1).astype(jnp.int32), (1,))
    smem = pl.BlockSpec(memory_space=pltpu.SMEM)
    vmem = pl.BlockSpec(memory_space=pltpu.VMEM)
    params = pltpu.CompilerParams(vmem_limit_bytes=48 << 20)

    target = (block_owner[:, 0] * 8 + block_cell).reshape(1, -1)
    half_shape = jax.ShapeDtypeStruct((4 * SLAB, HALF), jnp.float32)
    mine, theirs = pl.pallas_call(
        deliver_kernel,
        out_shape=(half_shape, half_shape),
        in_specs=[smem, vmem, vmem],
        out_specs=(vmem, vmem),
        scratch_shapes=[pltpu.VMEM((density.shape[0], WIDE), jnp.float32)],
        compiler_params=params,
        name="deliver",
    )(core, target, density)
    other = lax.ppermute(theirs, "band", [(i, i ^ 1) for i in range(band_count)])

    cells = jnp.transpose(orbitals, (1, 0, 2))
    scales = jnp.broadcast_to(cell_scale[:, None], (8, OWN))
    scales16 = jnp.concatenate([scales, scales], 0)[None]
    left = lax.ppermute(jnp.concatenate([cells[5:], scales16], 0), "dom", [(i, i + 1) for i in range(dom_count - 1)])
    right = lax.ppermute(jnp.concatenate([cells[:3], scales16], 0), "dom", [(i + 1, i) for i in range(dom_count - 1)])

    part = exchange((mine + other).reshape(4, SLAB, HALF), "dom", X_GROUPS)
    slab = jnp.sum(part, 0)
    windows = jnp.concatenate([slab[:128].reshape(16, 8, HALF), slab[8:].reshape(16, 8, HALF)], 1)
    part = exchange(windows, "dom", YZ_GROUPS)
    window = jnp.sum(part, 0)
    part = exchange(jnp.broadcast_to(window[None], (band_count, 16, HALF)), "band")
    rho = jnp.sum(part.reshape(4, 2, 16, HALF), 0)

    filtered = pl.pallas_call(
        filter_kernel,
        out_shape=jax.ShapeDtypeStruct((8, 16, OWN), jnp.float32),
        in_specs=[smem] + [vmem] * 6,
        out_specs=vmem,
        scratch_shapes=[
            pltpu.VMEM((WIDE, WIDE), jnp.float32),
            pltpu.VMEM((WIDE, WIDE), jnp.bfloat16),
            pltpu.VMEM((WIDE, WIDE), jnp.bfloat16),
            pltpu.VMEM((224, WIDE), jnp.float32),
            pltpu.VMEM((224, WIDE), jnp.float32),
            pltpu.VMEM((224, WIDE), jnp.float32),
            pltpu.VMEM((224, WIDE), jnp.bfloat16),
            pltpu.VMEM((224, WIDE), jnp.bfloat16),
            pltpu.VMEM((224, WIDE), jnp.float32),
            pltpu.VMEM((224, WIDE), jnp.float32),
            pltpu.VMEM((16, WIDE), jnp.float32),
        ],
        compiler_params=params,
        name="chebyshev",
    )(alive, cells, left, right, scales[:, :128], rho, cell_operator)

    flat = exchange(filtered, "band").reshape(128, OWN)
    total = OWN * dom_count * band_count
    gram = jnp.dot(flat, flat.T, precision=lax.Precision.HIGHEST)
    part = jnp.sum(exchange(gram.reshape(dom_count, 2, 128), "dom"), 0)
    part = jnp.sum(exchange(jnp.broadcast_to(part[None], (band_count, 2, 128)), "band"), 0)
    intersection = exchange(jnp.broadcast_to(part[None], (dom_count, 2, 128)), "dom").reshape(128, 128) / total
    lower = jnp.linalg.cholesky(intersection)
    basis = jax.scipy.linalg.solve_triangular(lower, flat, lower=True)
    return basis.reshape(128, 1, OWN)


def solution(mesh):
    return jax.shard_map(
        body,
        mesh=mesh,
        in_specs=(
            P("band", "dom", None),
            P(),
            P("dom"),
            P(("dom", "band"), None),
            P(("dom", "band"), None),
            P(("dom", "band")),
        ),
        out_specs=P(None, ("dom", "band"), None),
        check_vma=False,
    )
```

```python
import functools

import jax
import jax.numpy as jnp
from jax import lax
from jax.experimental import pallas as pl
from jax.experimental.pallas import tpu as pltpu
from jax.sharding import PartitionSpec as P

FACE = 81
OWN = 648
NODES = 729
WIDE = 768
HALF = 384
SLAB = 136
TILE5 = 640
SPLIT = OWN - TILE5

CENTER = -1.0
HALF_WIDTH = 2.5

X_GROUPS = [[x * 16 + r for x in range(4)] for r in range(16)]
YZ_GROUPS = [[x * 16 + r for r in range(16)] for x in range(4)]
XB_GROUPS = [[(x * 16 + r) * 8 + b for x in range(4) for b in range(8)] for r in range(16)]


def exchange(value, axis, groups=None):
    return lax.all_to_all(value, axis, split_axis=0, concat_axis=0, tiled=True, axis_index_groups=groups)


def split2(value):
    high = value.astype(jnp.bfloat16)
    low = (value - high.astype(jnp.float32)).astype(jnp.bfloat16)
    return high, low


def dot(a, b):
    return jnp.dot(a, b, preferred_element_type=jnp.float32)


def dot_nt(a, b):
    return lax.dot_general(a, b, (((1,), (1,)), ((), ())), preferred_element_type=jnp.float32)


def deliver_kernel(core_ref, owner_ref, cell_ref, density_ref, mine_ref, theirs_ref, wide_ref):
    rows = 4 * SLAB
    count = density_ref.shape[1]
    wide_ref[720:, :] = jnp.zeros((WIDE - 720, count), jnp.float32)
    wide_ref[:NODES, :] = density_ref[...]
    row = lax.broadcasted_iota(jnp.int32, (rows, count), 0)
    slab = (row >= SLAB).astype(jnp.int32) + (row >= 2 * SLAB).astype(jnp.int32) + (row >= 3 * SLAB).astype(jnp.int32)
    cell = row - 8 * slab - 3
    onehot = jnp.where(owner_ref[...] * 8 + cell_ref[...] == cell, 1.0, 0.0).astype(jnp.bfloat16)
    for half in range(2):
        values = wide_ref[half * HALF:(half + 1) * HALF, :]
        first = values.astype(jnp.bfloat16)
        rest = values - first.astype(jnp.float32)
        second = rest.astype(jnp.bfloat16)
        third = (rest - second.astype(jnp.float32)).astype(jnp.bfloat16)
        total = dot_nt(onehot, first) + dot_nt(onehot, second) + dot_nt(onehot, third)

        @pl.when(core_ref[0] == half)
        def _():
            mine_ref[...] = total

        @pl.when(core_ref[0] != half)
        def _():
            theirs_ref[...] = total


def prepare_kernel(scale_ref, orbitals_ref, operator_ref, cells_ref, left_ref, right_ref, khigh, klow, kwide):
    for c in range(8):
        value = orbitals_ref[:, c, :]
        cells_ref[c] = value
        if c >= 5:
            left_ref[c - 5] = value
        if c < 3:
            right_ref[c] = value
    for c in range(8):
        line = jnp.full((1, OWN), scale_ref[c], jnp.float32)
        left_ref[3, c:c + 1, :] = line
        right_ref[3, c:c + 1, :] = line
    left_ref[3, 8:, :] = jnp.zeros((8, OWN), jnp.float32)
    right_ref[3, 8:, :] = jnp.zeros((8, OWN), jnp.float32)
    kwide[720:, :] = jnp.zeros((WIDE - 720, WIDE), jnp.float32)
    kwide[:, TILE5:] = jnp.zeros((WIDE, WIDE - TILE5), jnp.float32)
    kwide[:NODES, :NODES] = operator_ref[...]
    for i in range(0, WIDE, 128):
        high, low = split2(kwide[i:i + 128, :])
        khigh[i:i + 128, :] = high
        klow[i:i + 128, :] = low


def filter_kernel(last_ref, scale_ref, own_ref, left_ref, right_ref, rho_ref, khigh, klow, out_ref,
                  v0, v1, v2, chigh, clow, cell_buf, product, pot):
    for half in range(2):
        rho = rho_ref[half]
        pot[:, half * HALF:(half + 1) * HALF] = jnp.where(
            rho > 0.0, -0.7386 * jnp.exp(jnp.log(jnp.where(rho > 0.0, rho, 1.0)) * (1.0 / 3.0)), 0.0)
    lane = lax.broadcasted_iota(jnp.int32, (16, 128), 1)
    is_face = lane < FACE
    is_own5 = lane < SPLIT
    zero5 = jnp.zeros((16, WIDE - TILE5), jnp.float32)

    def place(i, value):
        v0[16 * i:16 * i + 16, TILE5:] = zero5
        v0[16 * i:16 * i + 16, :OWN] = value

    for i in range(3):
        place(i, left_ref[i])
        place(11 + i, right_ref[i])
    for i in range(8):
        place(3 + i, own_ref[i])

    def scale_of(i):
        if i < 3:
            line = left_ref[3, 5 + i:6 + i, :128]
        elif i < 11:
            line = scale_ref[i - 3]
        else:
            line = right_ref[3, i - 11:i - 10, :128]
        return line

    alive = last_ref[0].astype(jnp.float32)

    def apply(source, begin, end, combine):
        for i in range(begin, end):
            r = slice(16 * i, 16 * i + 16)
            n = slice(16 * i + 16, 16 * i + 32)
            for t in range(6):
                c = slice(128 * t, 128 * t + 128)
                value = source[r, c]
                if t == 5:
                    face = jnp.where(is_face, source[n, :128], 0.0)
                    value = value + pltpu.roll(face, SPLIT, 1)
                cell_buf[r, c] = value
                high, low = split2(value)
                chigh[r, c] = high
                clow[r, c] = low
        r = slice(16 * begin, 16 * end)
        a, b = chigh[r, :], clow[r, :]
        product[r, :] = dot(a, khigh[...]) + dot(b, khigh[...]) + dot(a, klow[...])
        tail = None
        for i in range(begin, end):
            r = slice(16 * i, 16 * i + 16)
            scale = scale_of(i)
            parts = []
            for t in range(6):
                c = slice(128 * t, 128 * t + 128)
                parts.append(scale * product[r, c] + pot[i:i + 1, c] * cell_buf[r, c])
            if tail is not None:
                add = jnp.where(is_face, pltpu.roll(tail, 128 - SPLIT, 1), 0.0)
                if i == 11:
                    add = add * alive
                parts[0] = parts[0] + add
                for t in range(6):
                    value = parts[t]
                    if t == 5:
                        value = jnp.where(is_own5, value, 0.0)
                    combine(i, t, value)
            tail = parts[5]

    def at(ref, i, t):
        return ref[16 * i:16 * i + 16, 128 * t:128 * t + 128]

    def first(i, t, value):
        v1[16 * i:16 * i + 16, 128 * t:128 * t + 128] = (value - CENTER * at(v0, i, t)) * (1.0 / HALF_WIDTH)

    def second(i, t, value):
        v2[16 * i:16 * i + 16, 128 * t:128 * t + 128] = (value - CENTER * at(v1, i, t)) * (2.0 / HALF_WIDTH) - at(v0, i, t)

    def third(i, t, value):
        result = (value - CENTER * at(v2, i, t)) * (2.0 / HALF_WIDTH) - at(v1, i, t)
        if t < 5:
            out_ref[i - 3, :, 128 * t:128 * t + 128] = result
        else:
            out_ref[i - 3, :, TILE5:OWN] = result[:, :SPLIT]

    apply(v0, 0, 13, first)
    apply(v1, 1, 12, second)
    apply(v2, 2, 11, third)


def solve_kernel(total, gram_ref, flat_ref, out_ref, inverse_ref):
    shape = (8, 128)
    col = lax.broadcasted_iota(jnp.int32, shape, 1)
    row = lax.broadcasted_iota(jnp.int32, shape, 0)
    a = [gram_ref[8 * i:8 * i + 8, :] * (1.0 / total) for i in range(16)]
    w = [jnp.where(col == row + 8 * i, 1.0, 0.0) for i in range(16)]

    def columns(block, k):
        return [jnp.broadcast_to(block[:, 8 * k + j:8 * k + j + 1], shape) for j in range(8)]

    def line(block, i):
        return jnp.broadcast_to(block[i:i + 1, :], shape)

    for k in range(16):
        own = columns(a[k], k)
        s = [[line(own[j], i) for j in range(i + 1)] for i in range(8)]
        low = [[None] * 8 for _ in range(8)]
        inv = [None] * 8
        for j in range(8):
            inv[j] = 1.0 / s[j][j]
            for i in range(j + 1, 8):
                low[i][j] = s[i][j] * inv[j]
            for i in range(j + 1, 8):
                for m in range(j + 1, i + 1):
                    s[i][m] = s[i][m] - low[i][j] * s[m][j]
        n = [[None] * 8 for _ in range(8)]
        for i in range(8):
            for j in range(i):
                value = low[i][j]
                for m in range(j + 1, i):
                    value = value + low[i][m] * n[m][j]
                n[i][j] = -value

        def forward(block):
            lines = [line(block, i) for i in range(8)]
            result = []
            for i in range(8):
                value = lines[i]
                for j in range(i):
                    value = value + n[i][j] * lines[j]
                result.append(value)
            return result

        def backward(lines):
            scaled = [inv[i] * lines[i] for i in range(8)]
            result = []
            for j in range(8):
                value = scaled[j]
                for i in range(j + 1, 8):
                    value = value + n[i][j] * scaled[i]
                result.append(value)
            return result

        lines_w = forward(w[k])
        final = jnp.zeros(shape, jnp.float32)
        for i in range(8):
            final = jnp.where(row == i, lines_w[i] * jnp.sqrt(inv[i]), final)
        inverse_ref[8 * k:8 * k + 8, :] = final
        if k < 15:
            za = backward(forward(a[k]))
            zw = backward(lines_w)
            for i in range(k + 1, 16):
                c = columns(a[i], k)
                for j in range(8):
                    a[i] = a[i] - c[j] * za[j]
                    w[i] = w[i] - c[j] * zw[j]
    inverse_high, inverse_low = split2(inverse_ref[...])
    for begin in range(0, OWN, 128):
        c = slice(begin, min(begin + 128, OWN))
        flat_high, flat_low = split2(jnp.transpose(flat_ref[:, c]))
        out_ref[c, :] = (dot_nt(flat_high, inverse_high) + dot_nt(flat_low, inverse_high)
                         + dot_nt(flat_high, inverse_low))


def body(orbitals, cell_operator, cell_scale, density, block_owner, block_cell):
    dom_count = lax.axis_size("dom")
    band_count = lax.axis_size("band")
    dom = lax.axis_index("dom")
    core = jnp.reshape(lax.axis_index("band") % 2, (1,)).astype(jnp.int32)
    alive = jnp.reshape((dom < dom_count - 1).astype(jnp.int32), (1,))
    smem = pl.BlockSpec(memory_space=pltpu.SMEM)
    vmem = pl.BlockSpec(memory_space=pltpu.VMEM)
    params = pltpu.CompilerParams(vmem_limit_bytes=48 << 20)

    half_shape = jax.ShapeDtypeStruct((4 * SLAB, HALF), jnp.float32)
    mine, theirs = pl.pallas_call(
        deliver_kernel,
        out_shape=(half_shape, half_shape),
        in_specs=[smem, vmem, vmem, vmem],
        out_specs=(vmem, vmem),
        scratch_shapes=[pltpu.VMEM((WIDE, density.shape[0]), jnp.float32)],
        compiler_params=params,
        name="deliver",
    )(core, block_owner.reshape(1, -1), block_cell.reshape(1, -1), density.T)
    other = lax.ppermute(theirs, "band", [(i, i ^ 1) for i in range(band_count)])

    ghost_shape = jax.ShapeDtypeStruct((4, 16, OWN), jnp.float32)
    split_shape = jax.ShapeDtypeStruct((WIDE, WIDE), jnp.bfloat16)
    cells, send_left, send_right, khigh, klow = pl.pallas_call(
        prepare_kernel,
        out_shape=(jax.ShapeDtypeStruct((8, 16, OWN), jnp.float32), ghost_shape, ghost_shape, split_shape, split_shape),
        in_specs=[smem, vmem, vmem],
        out_specs=(vmem,) * 5,
        scratch_shapes=[pltpu.VMEM((WIDE, WIDE), jnp.float32)],
        compiler_params=params,
        name="prepare",
    )(cell_scale, orbitals, cell_operator)
    left = lax.ppermute(send_left, "dom", [(i, i + 1) for i in range(dom_count - 1)])
    right = lax.ppermute(send_right, "dom", [(i + 1, i) for i in range(dom_count - 1)])

    part = exchange((mine + other).reshape(4, SLAB, HALF), "dom", X_GROUPS)
    slab = jnp.sum(part, 0)
    windows = jnp.concatenate([slab[:128].reshape(16, 8, HALF), slab[8:].reshape(16, 8, HALF)], 1)
    part = exchange(windows, "dom", YZ_GROUPS)
    window = jnp.sum(part, 0)
    window, left, right = lax.optimization_barrier((window, left, right))
    part = exchange(jnp.broadcast_to(window[None], (band_count, 16, HALF)), "band")
    rho = jnp.sum(part.reshape(4, 2, 16, HALF), 0)

    filtered = pl.pallas_call(
        filter_kernel,
        out_shape=jax.ShapeDtypeStruct((8, 16, OWN), jnp.float32),
        in_specs=[smem] * 2 + [vmem] * 6,
        out_specs=vmem,
        scratch_shapes=[
            pltpu.VMEM((224, WIDE), jnp.float32),
            pltpu.VMEM((224, WIDE), jnp.float32),
            pltpu.VMEM((224, WIDE), jnp.float32),
            pltpu.VMEM((224, WIDE), jnp.bfloat16),
            pltpu.VMEM((224, WIDE), jnp.bfloat16),
            pltpu.VMEM((224, WIDE), jnp.float32),
            pltpu.VMEM((224, WIDE), jnp.float32),
            pltpu.VMEM((16, WIDE), jnp.float32),
        ],
        compiler_params=params,
        name="chebyshev",
    )(alive, cell_scale, cells, left, right, rho, khigh, klow)

    flat = exchange(filtered, "band").reshape(128, OWN)
    total = OWN * dom_count * band_count
    gram = jnp.dot(flat, flat.T, precision=lax.Precision.HIGHEST)
    part = jnp.sum(exchange(gram.reshape(16, 8, 128), "dom", YZ_GROUPS), 0)
    part = jnp.sum(exchange(jnp.broadcast_to(part[None], (32, 8, 128)), ("dom", "band"), XB_GROUPS), 0)
    gram = exchange(jnp.broadcast_to(part[None], (16, 8, 128)), "dom", YZ_GROUPS).reshape(128, 128)
    basis = pl.pallas_call(
        functools.partial(solve_kernel, float(total)),
        out_shape=jax.ShapeDtypeStruct((OWN, 128), jnp.float32),
        in_specs=[vmem, vmem],
        out_specs=vmem,
        scratch_shapes=[pltpu.VMEM((128, 128), jnp.float32)],
        compiler_params=params,
        name="orthonormalize",
    )(gram, flat)
    return basis.T.reshape(128, 1, OWN)


def solution(mesh):
    return jax.shard_map(
        body,
        mesh=mesh,
        in_specs=(
            P("band", "dom", None),
            P(),
            P("dom"),
            P(("dom", "band"), None),
            P(("dom", "band"), None),
            P(("dom", "band")),
        ),
        out_specs=P(None, ("dom", "band"), None),
        check_vma=False,
    )
```

```python
import functools

import jax
import jax.numpy as jnp
from jax import lax
from jax.experimental import pallas as pl
from jax.experimental.pallas import tpu as pltpu
from jax.sharding import PartitionSpec as P

FACE = 81
OWN = 648
NODES = 729
WIDE = 768
HALF = 384
SLAB = 136
TILE5 = 640
SPLIT = OWN - TILE5

CENTER = -1.0
HALF_WIDTH = 2.5

X_GROUPS = [[x * 16 + r for x in range(4)] for r in range(16)]
YZ_GROUPS = [[x * 16 + r for r in range(16)] for x in range(4)]
XB_GROUPS = [[(x * 16 + r) * 8 + b for x in range(4) for b in range(8)] for r in range(16)]


def exchange(value, axis, groups=None):
    return lax.all_to_all(value, axis, split_axis=0, concat_axis=0, tiled=True, axis_index_groups=groups)


def split2(value):
    high = value.astype(jnp.bfloat16)
    low = (value - high.astype(jnp.float32)).astype(jnp.bfloat16)
    return high, low


def dot(a, b):
    return jnp.dot(a, b, preferred_element_type=jnp.float32)


def dot_nt(a, b):
    return lax.dot_general(a, b, (((1,), (1,)), ((), ())), preferred_element_type=jnp.float32)


def deliver_kernel(core_ref, owner_hbm, cell_hbm, density_hbm, mine_ref, theirs_ref,
                   owner_ref, cell_ref, density_ref, wide_ref, sems):
    rows = 4 * SLAB
    count = density_ref.shape[1]
    copies = [
        pltpu.make_async_copy(density_hbm, density_ref, sems.at[0]),
        pltpu.make_async_copy(owner_hbm, owner_ref, sems.at[1]),
        pltpu.make_async_copy(cell_hbm, cell_ref, sems.at[2]),
    ]
    for copy in copies:
        copy.start()
    wide_ref[720:, :] = jnp.zeros((WIDE - 720, count), jnp.float32)
    for copy in copies:
        copy.wait()
    wide_ref[:NODES, :] = density_ref[...]
    row = lax.broadcasted_iota(jnp.int32, (rows, count), 0)
    slab = (row >= SLAB).astype(jnp.int32) + (row >= 2 * SLAB).astype(jnp.int32) + (row >= 3 * SLAB).astype(jnp.int32)
    cell = row - 8 * slab - 3
    onehot = jnp.where(owner_ref[...] * 8 + cell_ref[...] == cell, 1.0, 0.0).astype(jnp.bfloat16)
    for half in range(2):
        values = wide_ref[half * HALF:(half + 1) * HALF, :]
        first = values.astype(jnp.bfloat16)
        rest = values - first.astype(jnp.float32)
        second = rest.astype(jnp.bfloat16)
        third = (rest - second.astype(jnp.float32)).astype(jnp.bfloat16)
        total = dot_nt(onehot, first) + dot_nt(onehot, second) + dot_nt(onehot, third)

        @pl.when(core_ref[0] == half)
        def _():
            mine_ref[...] = total

        @pl.when(core_ref[0] != half)
        def _():
            theirs_ref[...] = total


def prepare_kernel(scale_ref, orbitals_ref, operator_ref, left_ref, right_ref, khigh, klow, kwide):
    for c in range(3):
        left_ref[c] = orbitals_ref[:, 5 + c, :]
        right_ref[c] = orbitals_ref[:, c, :]
    for c in range(8):
        line = jnp.full((1, OWN), scale_ref[c], jnp.float32)
        left_ref[3, c:c + 1, :] = line
        right_ref[3, c:c + 1, :] = line
    left_ref[3, 8:, :] = jnp.zeros((8, OWN), jnp.float32)
    right_ref[3, 8:, :] = jnp.zeros((8, OWN), jnp.float32)
    kwide[720:, :] = jnp.zeros((WIDE - 720, WIDE), jnp.float32)
    kwide[:, TILE5:] = jnp.zeros((WIDE, WIDE - TILE5), jnp.float32)
    kwide[:NODES, :NODES] = operator_ref[...]
    for i in range(0, WIDE, 128):
        high, low = split2(kwide[i:i + 128, :])
        khigh[i:i + 128, :] = high
        klow[i:i + 128, :] = low


def filter_kernel(last_ref, scale_ref, own_ref, left_ref, right_ref, rho_ref, khigh_hbm, klow_hbm, out_ref,
                  khigh, klow, ksems, v0, v1, v2, chigh, clow, cell_buf, product, pot):
    copies = [
        pltpu.make_async_copy(khigh_hbm, khigh, ksems.at[0]),
        pltpu.make_async_copy(klow_hbm, klow, ksems.at[1]),
    ]
    for copy in copies:
        copy.start()
    for half in range(2):
        rho = rho_ref[half]
        pot[:, half * HALF:(half + 1) * HALF] = jnp.where(
            rho > 0.0, -0.7386 * jnp.exp(jnp.log(jnp.where(rho > 0.0, rho, 1.0)) * (1.0 / 3.0)), 0.0)
    lane = lax.broadcasted_iota(jnp.int32, (16, 128), 1)
    is_face = lane < FACE
    is_own5 = lane < SPLIT
    zero5 = jnp.zeros((16, WIDE - TILE5), jnp.float32)

    def place(i, value):
        v0[16 * i:16 * i + 16, TILE5:] = zero5
        v0[16 * i:16 * i + 16, :OWN] = value

    for i in range(3):
        place(i, left_ref[i])
        place(11 + i, right_ref[i])
    for i in range(8):
        place(3 + i, own_ref[:, i, :])

    def scale_of(i):
        if i < 3:
            line = left_ref[3, 5 + i:6 + i, :128]
        elif i < 11:
            line = scale_ref[i - 3]
        else:
            line = right_ref[3, i - 11:i - 10, :128]
        return line

    alive = last_ref[0].astype(jnp.float32)

    def apply(source, begin, end, combine):
        for i in range(begin, end):
            r = slice(16 * i, 16 * i + 16)
            n = slice(16 * i + 16, 16 * i + 32)
            for t in range(6):
                c = slice(128 * t, 128 * t + 128)
                value = source[r, c]
                if t == 5:
                    face = jnp.where(is_face, source[n, :128], 0.0)
                    value = value + pltpu.roll(face, SPLIT, 1)
                cell_buf[r, c] = value
                high, low = split2(value)
                chigh[r, c] = high
                clow[r, c] = low
        r = slice(16 * begin, 16 * end)
        a, b = chigh[r, :], clow[r, :]
        if begin == 0:
            for copy in copies:
                copy.wait()
        product[r, :] = dot(a, khigh[...]) + dot(b, khigh[...]) + dot(a, klow[...])
        tail = None
        for i in range(begin, end):
            r = slice(16 * i, 16 * i + 16)
            scale = scale_of(i)
            parts = []
            for t in range(6):
                c = slice(128 * t, 128 * t + 128)
                parts.append(scale * product[r, c] + pot[i:i + 1, c] * cell_buf[r, c])
            if tail is not None:
                add = jnp.where(is_face, pltpu.roll(tail, 128 - SPLIT, 1), 0.0)
                if i == 11:
                    add = add * alive
                parts[0] = parts[0] + add
                for t in range(6):
                    value = parts[t]
                    if t == 5:
                        value = jnp.where(is_own5, value, 0.0)
                    combine(i, t, value)
            tail = parts[5]

    def at(ref, i, t):
        return ref[16 * i:16 * i + 16, 128 * t:128 * t + 128]

    def first(i, t, value):
        v1[16 * i:16 * i + 16, 128 * t:128 * t + 128] = (value - CENTER * at(v0, i, t)) * (1.0 / HALF_WIDTH)

    def second(i, t, value):
        v2[16 * i:16 * i + 16, 128 * t:128 * t + 128] = (value - CENTER * at(v1, i, t)) * (2.0 / HALF_WIDTH) - at(v0, i, t)

    def third(i, t, value):
        result = (value - CENTER * at(v2, i, t)) * (2.0 / HALF_WIDTH) - at(v1, i, t)
        if t < 5:
            out_ref[i - 3, :, 128 * t:128 * t + 128] = result
        else:
            out_ref[i - 3, :, TILE5:OWN] = result[:, :SPLIT]

    apply(v0, 0, 13, first)
    apply(v1, 1, 12, second)
    apply(v2, 2, 11, third)


def solve_kernel(total, gram_ref, flat_ref, out_ref, inverse_ref):
    shape = (8, 128)
    col = lax.broadcasted_iota(jnp.int32, shape, 1)
    row = lax.broadcasted_iota(jnp.int32, shape, 0)
    a = [gram_ref[8 * i:8 * i + 8, :] * (1.0 / total) for i in range(16)]
    w = [jnp.where(col == row + 8 * i, 1.0, 0.0) for i in range(16)]

    def columns(block, k):
        return [jnp.broadcast_to(block[:, 8 * k + j:8 * k + j + 1], shape) for j in range(8)]

    def line(block, i):
        return jnp.broadcast_to(block[i:i + 1, :], shape)

    for k in range(16):
        own = columns(a[k], k)
        s = [[line(own[j], i) for j in range(i + 1)] for i in range(8)]
        low = [[None] * 8 for _ in range(8)]
        inv = [None] * 8
        for j in range(8):
            inv[j] = 1.0 / s[j][j]
            for i in range(j + 1, 8):
                low[i][j] = s[i][j] * inv[j]
            for i in range(j + 1, 8):
                for m in range(j + 1, i + 1):
                    s[i][m] = s[i][m] - low[i][j] * s[m][j]
        n = [[None] * 8 for _ in range(8)]
        for i in range(8):
            for j in range(i):
                value = low[i][j]
                for m in range(j + 1, i):
                    value = value + low[i][m] * n[m][j]
                n[i][j] = -value

        def forward(block):
            lines = [line(block, i) for i in range(8)]
            result = []
            for i in range(8):
                value = lines[i]
                for j in range(i):
                    value = value + n[i][j] * lines[j]
                result.append(value)
            return result

        def backward(lines):
            scaled = [inv[i] * lines[i] for i in range(8)]
            result = []
            for j in range(8):
                value = scaled[j]
                for i in range(j + 1, 8):
                    value = value + n[i][j] * scaled[i]
                result.append(value)
            return result

        lines_w = forward(w[k])
        final = jnp.zeros(shape, jnp.float32)
        for i in range(8):
            final = jnp.where(row == i, lines_w[i] * jnp.sqrt(inv[i]), final)
        inverse_ref[8 * k:8 * k + 8, :] = final
        if k < 15:
            za = backward(forward(a[k]))
            zw = backward(lines_w)
            for i in range(k + 1, 16):
                c = columns(a[i], k)
                for j in range(8):
                    a[i] = a[i] - c[j] * za[j]
                    w[i] = w[i] - c[j] * zw[j]
    inverse_high, inverse_low = split2(inverse_ref[...])
    for begin in range(0, OWN, 128):
        c = slice(begin, min(begin + 128, OWN))
        flat_high, flat_low = split2(jnp.transpose(flat_ref[:, c]))
        out_ref[c, :] = (dot_nt(flat_high, inverse_high) + dot_nt(flat_low, inverse_high)
                         + dot_nt(flat_high, inverse_low))


def body(orbitals, cell_operator, cell_scale, density, block_owner, block_cell):
    dom_count = lax.axis_size("dom")
    band_count = lax.axis_size("band")
    dom = lax.axis_index("dom")
    core = jnp.reshape(lax.axis_index("band") % 2, (1,)).astype(jnp.int32)
    alive = jnp.reshape((dom < dom_count - 1).astype(jnp.int32), (1,))
    smem = pl.BlockSpec(memory_space=pltpu.SMEM)
    vmem = pl.BlockSpec(memory_space=pltpu.VMEM)
    hbm = pl.BlockSpec(memory_space=pltpu.HBM)
    params = pltpu.CompilerParams(vmem_limit_bytes=16 << 20)
    roomy = pltpu.CompilerParams(vmem_limit_bytes=62 << 20)

    half_shape = jax.ShapeDtypeStruct((4 * SLAB, HALF), jnp.float32)
    mine, theirs = pl.pallas_call(
        deliver_kernel,
        out_shape=(half_shape, half_shape),
        in_specs=[smem, hbm, hbm, hbm],
        out_specs=(vmem, vmem),
        scratch_shapes=[
            pltpu.VMEM((1, density.shape[0]), jnp.int32),
            pltpu.VMEM((1, density.shape[0]), jnp.int32),
            pltpu.VMEM((NODES, density.shape[0]), jnp.float32),
            pltpu.VMEM((WIDE, density.shape[0]), jnp.float32),
            pltpu.SemaphoreType.DMA((3,)),
        ],
        compiler_params=roomy,
        name="deliver",
    )(core, block_owner.reshape(1, -1), block_cell.reshape(1, -1), density.T)
    other = lax.ppermute(theirs, "band", [(i, i ^ 1) for i in range(band_count)])

    ghost_shape = jax.ShapeDtypeStruct((4, 16, OWN), jnp.float32)
    split_shape = jax.ShapeDtypeStruct((WIDE, WIDE), jnp.bfloat16)
    send_left, send_right, khigh, klow = pl.pallas_call(
        prepare_kernel,
        out_shape=(ghost_shape, ghost_shape, split_shape, split_shape),
        in_specs=[smem, vmem, vmem],
        out_specs=(vmem,) * 4,
        scratch_shapes=[pltpu.VMEM((WIDE, WIDE), jnp.float32)],
        compiler_params=params,
        name="prepare",
    )(cell_scale, orbitals, cell_operator)
    left = lax.ppermute(send_left, "dom", [(i, i + 1) for i in range(dom_count - 1)])
    right = lax.ppermute(send_right, "dom", [(i + 1, i) for i in range(dom_count - 1)])

    part = exchange((mine + other).reshape(4, SLAB, HALF), "dom", X_GROUPS)
    slab = jnp.sum(part, 0)
    windows = jnp.concatenate([slab[:128].reshape(16, 8, HALF), slab[8:].reshape(16, 8, HALF)], 1)
    windows, left, right = lax.optimization_barrier((windows, left, right))
    part = exchange(windows, "dom", YZ_GROUPS)
    window = jnp.sum(part, 0)
    part = exchange(jnp.broadcast_to(window[None], (band_count, 16, HALF)), "band")
    rho = jnp.sum(part.reshape(4, 2, 16, HALF), 0)

    filtered = pl.pallas_call(
        filter_kernel,
        out_shape=jax.ShapeDtypeStruct((8, 16, OWN), jnp.float32),
        in_specs=[smem] * 2 + [vmem] * 4 + [hbm] * 2,
        out_specs=vmem,
        scratch_shapes=[
            pltpu.VMEM((WIDE, WIDE), jnp.bfloat16),
            pltpu.VMEM((WIDE, WIDE), jnp.bfloat16),
            pltpu.SemaphoreType.DMA((2,)),
            pltpu.VMEM((224, WIDE), jnp.float32),
            pltpu.VMEM((224, WIDE), jnp.float32),
            pltpu.VMEM((224, WIDE), jnp.float32),
            pltpu.VMEM((224, WIDE), jnp.bfloat16),
            pltpu.VMEM((224, WIDE), jnp.bfloat16),
            pltpu.VMEM((224, WIDE), jnp.float32),
            pltpu.VMEM((224, WIDE), jnp.float32),
            pltpu.VMEM((16, WIDE), jnp.float32),
        ],
        compiler_params=roomy,
        name="chebyshev",
    )(alive, cell_scale, orbitals, left, right, rho, khigh, klow)

    flat = exchange(filtered, "band").reshape(128, OWN)
    total = OWN * dom_count * band_count
    gram = jnp.dot(flat, flat.T, precision=lax.Precision.HIGHEST)
    part = jnp.sum(exchange(gram.reshape(16, 8, 128), "dom", YZ_GROUPS), 0)
    part = jnp.sum(exchange(jnp.broadcast_to(part[None], (32, 8, 128)), ("dom", "band"), XB_GROUPS), 0)
    gram = exchange(jnp.broadcast_to(part[None], (16, 8, 128)), "dom", YZ_GROUPS).reshape(128, 128)
    basis = pl.pallas_call(
        functools.partial(solve_kernel, float(total)),
        out_shape=jax.ShapeDtypeStruct((OWN, 128), jnp.float32),
        in_specs=[vmem, vmem],
        out_specs=vmem,
        scratch_shapes=[pltpu.VMEM((128, 128), jnp.float32)],
        compiler_params=params,
        name="orthonormalize",
    )(gram, flat)
    return basis.T.reshape(128, 1, OWN)


def solution(mesh):
    return jax.shard_map(
        body,
        mesh=mesh,
        in_specs=(
            P("band", "dom", None),
            P(),
            P("dom"),
            P(("dom", "band"), None),
            P(("dom", "band"), None),
            P(("dom", "band")),
        ),
        out_specs=P(None, ("dom", "band"), None),
        check_vma=False,
    )
```

```python
import functools

import jax
import jax.numpy as jnp
from jax import lax
from jax.experimental import pallas as pl
from jax.experimental.pallas import tpu as pltpu
from jax.sharding import PartitionSpec as P

FACE = 81
OWN = 648
NODES = 729
WIDE = 768
HALF = 384
SLAB = 136
TILE5 = 640
SPLIT = OWN - TILE5

CENTER = -1.0
HALF_WIDTH = 2.5

X_GROUPS = [[x * 16 + r for x in range(4)] for r in range(16)]
YZ_GROUPS = [[x * 16 + r for r in range(16)] for x in range(4)]
XB_GROUPS = [[(x * 16 + r) * 8 + b for x in range(4) for b in range(8)] for r in range(16)]


def exchange(value, axis, groups=None):
    return lax.all_to_all(value, axis, split_axis=0, concat_axis=0, tiled=True, axis_index_groups=groups)


def split2(value):
    high = value.astype(jnp.bfloat16)
    low = (value - high.astype(jnp.float32)).astype(jnp.bfloat16)
    return high, low


def dot(a, b):
    return jnp.dot(a, b, preferred_element_type=jnp.float32)


def dot_nt(a, b):
    return lax.dot_general(a, b, (((1,), (1,)), ((), ())), preferred_element_type=jnp.float32)


def pack_kernel(core_ref, owner_hbm, cell_hbm, density_hbm, scale_hbm, orbitals_hbm,
                own_ref, send_ref, left_ref, right_ref,
                owner_ref, cell_ref, density_ref, scale_ref, orbitals_ref, sems):
    copies = [
        pltpu.make_async_copy(density_hbm, density_ref, sems.at[0]),
        pltpu.make_async_copy(owner_hbm, owner_ref, sems.at[1]),
        pltpu.make_async_copy(cell_hbm, cell_ref, sems.at[2]),
        pltpu.make_async_copy(scale_hbm, scale_ref, sems.at[3]),
        pltpu.make_async_copy(orbitals_hbm, orbitals_ref, sems.at[4]),
    ]
    for copy in copies:
        copy.start()
    for copy in copies:
        copy.wait()
    for c in range(3):
        left_ref[c] = orbitals_ref[:, 5 + c, :]
        right_ref[c] = orbitals_ref[:, c, :]
    diagonal = lax.broadcasted_iota(jnp.int32, (8, 8), 0) == lax.broadcasted_iota(jnp.int32, (8, 8), 1)
    column = jnp.sum(jnp.where(diagonal, jnp.broadcast_to(scale_ref[...], (8, 8)), 0.0), 1, keepdims=True)
    for ref in (left_ref, right_ref):
        ref[3, :8, :] = jnp.broadcast_to(column, (8, OWN))
        ref[3, 8:, :] = jnp.zeros((8, OWN), jnp.float32)
    count = density_ref.shape[1]
    target = (owner_ref[...] * 8 + cell_ref[...]).astype(jnp.float32)
    target = jnp.broadcast_to(target, (8, count))

    def lower(ref):
        ref[:HALF, :] = density_ref[:HALF, :]
        ref[HALF:, :] = target

    def upper(ref):
        ref[:344, :] = density_ref[HALF:728, :]
        ref[344:HALF, :] = jnp.zeros((HALF - 344, count), jnp.float32)
        ref[344:345, :] = density_ref[728:NODES, :]
        ref[HALF:, :] = target

    @pl.when(core_ref[0] == 0)
    def _():
        lower(own_ref)
        upper(send_ref)

    @pl.when(core_ref[0] != 0)
    def _():
        upper(own_ref)
        lower(send_ref)


def deliver_kernel(own_ref, other_ref, out_ref):
    rows = 4 * SLAB
    count = own_ref.shape[1]
    row = lax.broadcasted_iota(jnp.int32, (rows, count), 0)
    slab = (row >= SLAB).astype(jnp.int32) + (row >= 2 * SLAB).astype(jnp.int32) + (row >= 3 * SLAB).astype(jnp.int32)
    cell = (row - 8 * slab - 3).astype(jnp.float32)
    total = None
    for ref in (own_ref, other_ref):
        onehot = jnp.where(ref[HALF:HALF + 1, :] == cell, 1.0, 0.0).astype(jnp.bfloat16)
        values = ref[:HALF, :]
        first = values.astype(jnp.bfloat16)
        rest = values - first.astype(jnp.float32)
        second = rest.astype(jnp.bfloat16)
        third = (rest - second.astype(jnp.float32)).astype(jnp.bfloat16)
        part = dot_nt(onehot, first) + dot_nt(onehot, second) + dot_nt(onehot, third)
        total = part if total is None else total + part
    out_ref[...] = total


def window_kernel(part_ref, out_ref):
    for k in range(17):
        r = slice(8 * k, 8 * k + 8)
        block = (part_ref[0, r, :] + part_ref[1, r, :]) + (part_ref[2, r, :] + part_ref[3, r, :])
        if k < 16:
            out_ref[k, :8, :] = block
        if k > 0:
            out_ref[k - 1, 8:, :] = block


def filter_kernel(last_ref, scale_ref, own_ref, left_ref, right_ref, part_ref, operator_ref, out_ref,
                  kwide, khigh, klow, v0, v1, v2, chigh, clow, cell_buf, product, pot):
    kwide[720:, :] = jnp.zeros((WIDE - 720, WIDE), jnp.float32)
    kwide[:, TILE5:] = jnp.zeros((WIDE, WIDE - TILE5), jnp.float32)
    kwide[:NODES, :NODES] = operator_ref[...]
    for i in range(0, WIDE, 128):
        high, low = split2(kwide[i:i + 128, :])
        khigh[i:i + 128, :] = high
        klow[i:i + 128, :] = low
    for half in range(2):
        rho = (part_ref[half] + part_ref[half + 2]) + (part_ref[half + 4] + part_ref[half + 6])
        pot[:, half * HALF:(half + 1) * HALF] = jnp.where(
            rho > 0.0, -0.7386 * jnp.exp(jnp.log(jnp.where(rho > 0.0, rho, 1.0)) * (1.0 / 3.0)), 0.0)
    lane = lax.broadcasted_iota(jnp.int32, (16, 128), 1)
    is_face = lane < FACE
    is_own5 = lane < SPLIT
    zero5 = jnp.zeros((16, WIDE - TILE5), jnp.float32)

    def place(i, value):
        v0[16 * i:16 * i + 16, TILE5:] = zero5
        v0[16 * i:16 * i + 16, :OWN] = value

    for i in range(3):
        place(i, left_ref[i])
        place(11 + i, right_ref[i])
    for i in range(8):
        place(3 + i, own_ref[:, i, :])

    def scale_of(i):
        if i < 3:
            line = left_ref[3, 5 + i:6 + i, :128]
        elif i < 11:
            line = scale_ref[i - 3]
        else:
            line = right_ref[3, i - 11:i - 10, :128]
        return line

    alive = last_ref[0].astype(jnp.float32)

    def apply(source, begin, end, combine):
        for i in range(begin, end):
            r = slice(16 * i, 16 * i + 16)
            n = slice(16 * i + 16, 16 * i + 32)
            for t in range(6):
                c = slice(128 * t, 128 * t + 128)
                value = source[r, c]
                if t == 5:
                    face = jnp.where(is_face, source[n, :128], 0.0)
                    value = value + pltpu.roll(face, SPLIT, 1)
                cell_buf[r, c] = value
                high, low = split2(value)
                chigh[r, c] = high
                clow[r, c] = low
        r = slice(16 * begin, 16 * end)
        a, b = chigh[r, :], clow[r, :]
        product[r, :] = dot(a, khigh[...]) + dot(b, khigh[...]) + dot(a, klow[...])
        tail = None
        for i in range(begin, end):
            r = slice(16 * i, 16 * i + 16)
            scale = scale_of(i)
            parts = []
            for t in range(6):
                c = slice(128 * t, 128 * t + 128)
                parts.append(scale * product[r, c] + pot[i:i + 1, c] * cell_buf[r, c])
            if tail is not None:
                add = jnp.where(is_face, pltpu.roll(tail, 128 - SPLIT, 1), 0.0)
                if i == 11:
                    add = add * alive
                parts[0] = parts[0] + add
                for t in range(6):
                    value = parts[t]
                    if t == 5:
                        value = jnp.where(is_own5, value, 0.0)
                    combine(i, t, value)
            tail = parts[5]

    def at(ref, i, t):
        return ref[16 * i:16 * i + 16, 128 * t:128 * t + 128]

    def first(i, t, value):
        v1[16 * i:16 * i + 16, 128 * t:128 * t + 128] = (value - CENTER * at(v0, i, t)) * (1.0 / HALF_WIDTH)

    def second(i, t, value):
        v2[16 * i:16 * i + 16, 128 * t:128 * t + 128] = (value - CENTER * at(v1, i, t)) * (2.0 / HALF_WIDTH) - at(v0, i, t)

    def third(i, t, value):
        result = (value - CENTER * at(v2, i, t)) * (2.0 / HALF_WIDTH) - at(v1, i, t)
        if t < 5:
            out_ref[i - 3, :, 128 * t:128 * t + 128] = result
        else:
            out_ref[i - 3, :, TILE5:OWN] = result[:, :SPLIT]

    apply(v0, 0, 13, first)
    apply(v1, 1, 12, second)
    apply(v2, 2, 11, third)


def solve_kernel(total, gram_ref, flat_ref, out_ref, inverse_ref):
    shape = (8, 128)
    col = lax.broadcasted_iota(jnp.int32, shape, 1)
    row = lax.broadcasted_iota(jnp.int32, shape, 0)
    a = [gram_ref[8 * i:8 * i + 8, :] * (1.0 / total) for i in range(16)]
    w = [jnp.where(col == row + 8 * i, 1.0, 0.0) for i in range(16)]

    def columns(block, k):
        return [jnp.broadcast_to(block[:, 8 * k + j:8 * k + j + 1], shape) for j in range(8)]

    def line(block, i):
        return jnp.broadcast_to(block[i:i + 1, :], shape)

    for k in range(16):
        own = columns(a[k], k)
        s = [[line(own[j], i) for j in range(i + 1)] for i in range(8)]
        low = [[None] * 8 for _ in range(8)]
        inv = [None] * 8
        for j in range(8):
            inv[j] = 1.0 / s[j][j]
            for i in range(j + 1, 8):
                low[i][j] = s[i][j] * inv[j]
            for i in range(j + 1, 8):
                for m in range(j + 1, i + 1):
                    s[i][m] = s[i][m] - low[i][j] * s[m][j]
        n = [[None] * 8 for _ in range(8)]
        for i in range(8):
            for j in range(i):
                value = low[i][j]
                for m in range(j + 1, i):
                    value = value + low[i][m] * n[m][j]
                n[i][j] = -value

        def forward(block):
            lines = [line(block, i) for i in range(8)]
            result = []
            for i in range(8):
                value = lines[i]
                for j in range(i):
                    value = value + n[i][j] * lines[j]
                result.append(value)
            return result

        def backward(lines):
            scaled = [inv[i] * lines[i] for i in range(8)]
            result = []
            for j in range(8):
                value = scaled[j]
                for i in range(j + 1, 8):
                    value = value + n[i][j] * scaled[i]
                result.append(value)
            return result

        lines_w = forward(w[k])
        final = jnp.zeros(shape, jnp.float32)
        for i in range(8):
            final = jnp.where(row == i, lines_w[i] * jnp.sqrt(inv[i]), final)
        inverse_ref[8 * k:8 * k + 8, :] = final
        if k < 15:
            za = backward(forward(a[k]))
            zw = backward(lines_w)
            for i in range(k + 1, 16):
                c = columns(a[i], k)
                for j in range(8):
                    a[i] = a[i] - c[j] * za[j]
                    w[i] = w[i] - c[j] * zw[j]
    inverse_high, inverse_low = split2(inverse_ref[...])
    for begin in range(0, OWN, 128):
        c = slice(begin, min(begin + 128, OWN))
        flat_high, flat_low = split2(jnp.transpose(flat_ref[:, c]))
        out_ref[c, :] = (dot_nt(flat_high, inverse_high) + dot_nt(flat_low, inverse_high)
                         + dot_nt(flat_high, inverse_low))


def body(orbitals, cell_operator, cell_scale, density, block_owner, block_cell):
    dom_count = lax.axis_size("dom")
    band_count = lax.axis_size("band")
    dom = lax.axis_index("dom")
    core = jnp.reshape(lax.axis_index("band") % 2, (1,)).astype(jnp.int32)
    alive = jnp.reshape((dom < dom_count - 1).astype(jnp.int32), (1,))
    smem = pl.BlockSpec(memory_space=pltpu.SMEM)
    vmem = pl.BlockSpec(memory_space=pltpu.VMEM)
    hbm = pl.BlockSpec(memory_space=pltpu.HBM)
    params = pltpu.CompilerParams(vmem_limit_bytes=16 << 20)
    roomy = pltpu.CompilerParams(vmem_limit_bytes=62 << 20)

    count = density.shape[0]
    pack_shape = jax.ShapeDtypeStruct((HALF + 8, count), jnp.float32)
    ghost_shape = jax.ShapeDtypeStruct((4, 16, OWN), jnp.float32)
    own, send, send_left, send_right = pl.pallas_call(
        pack_kernel,
        out_shape=(pack_shape, pack_shape, ghost_shape, ghost_shape),
        in_specs=[smem] + [hbm] * 5,
        out_specs=(vmem,) * 4,
        scratch_shapes=[
            pltpu.VMEM((1, count), jnp.int32),
            pltpu.VMEM((1, count), jnp.int32),
            pltpu.VMEM((NODES, count), jnp.float32),
            pltpu.VMEM((1, 8), jnp.float32),
            pltpu.VMEM((16, 8, OWN), jnp.float32),
            pltpu.SemaphoreType.DMA((5,)),
        ],
        compiler_params=roomy,
        name="pack",
    )(core, block_owner.reshape(1, -1), block_cell.reshape(1, -1), density.T, cell_scale.reshape(1, -1), orbitals)
    other = lax.ppermute(send, "band", [(i, i ^ 1) for i in range(band_count)])
    delivered = pl.pallas_call(
        deliver_kernel,
        out_shape=jax.ShapeDtypeStruct((4 * SLAB, HALF), jnp.float32),
        in_specs=[vmem, vmem],
        out_specs=vmem,
        compiler_params=params,
        name="deliver",
    )(own, other)

    left = lax.ppermute(send_left, "dom", [(i, i + 1) for i in range(dom_count - 1)])
    right = lax.ppermute(send_right, "dom", [(i + 1, i) for i in range(dom_count - 1)])

    part = exchange(delivered.reshape(4, SLAB, HALF), "dom", X_GROUPS)
    windows = pl.pallas_call(
        window_kernel,
        out_shape=jax.ShapeDtypeStruct((16, 16, HALF), jnp.float32),
        in_specs=[vmem],
        out_specs=vmem,
        compiler_params=params,
        name="windows",
    )(part)
    windows, left, right = lax.optimization_barrier((windows, left, right))
    part = exchange(windows, "dom", YZ_GROUPS)
    window = jnp.sum(part, 0)
    part = exchange(jnp.broadcast_to(window[None], (band_count, 16, HALF)), "band")

    filtered = pl.pallas_call(
        filter_kernel,
        out_shape=jax.ShapeDtypeStruct((8, 16, OWN), jnp.float32),
        in_specs=[smem] * 2 + [vmem] * 5,
        out_specs=vmem,
        scratch_shapes=[
            pltpu.VMEM((WIDE, WIDE), jnp.float32),
            pltpu.VMEM((WIDE, WIDE), jnp.bfloat16),
            pltpu.VMEM((WIDE, WIDE), jnp.bfloat16),
            pltpu.VMEM((224, WIDE), jnp.float32),
            pltpu.VMEM((224, WIDE), jnp.float32),
            pltpu.VMEM((224, WIDE), jnp.float32),
            pltpu.VMEM((224, WIDE), jnp.bfloat16),
            pltpu.VMEM((224, WIDE), jnp.bfloat16),
            pltpu.VMEM((224, WIDE), jnp.float32),
            pltpu.VMEM((224, WIDE), jnp.float32),
            pltpu.VMEM((16, WIDE), jnp.float32),
        ],
        compiler_params=params,
        name="chebyshev",
    )(alive, cell_scale, orbitals, left, right, part, cell_operator)

    flat = exchange(filtered, "band").reshape(128, OWN)
    total = OWN * dom_count * band_count
    gram = jnp.dot(flat, flat.T, precision=lax.Precision.HIGHEST)
    part = jnp.sum(exchange(gram.reshape(16, 8, 128), "dom", YZ_GROUPS), 0)
    part = jnp.sum(exchange(jnp.broadcast_to(part[None], (32, 8, 128)), ("dom", "band"), XB_GROUPS), 0)
    gram = exchange(jnp.broadcast_to(part[None], (16, 8, 128)), "dom", YZ_GROUPS).reshape(128, 128)
    basis = pl.pallas_call(
        functools.partial(solve_kernel, float(total)),
        out_shape=jax.ShapeDtypeStruct((OWN, 128), jnp.float32),
        in_specs=[vmem, vmem],
        out_specs=vmem,
        scratch_shapes=[pltpu.VMEM((128, 128), jnp.float32)],
        compiler_params=params,
        name="orthonormalize",
    )(gram, flat)
    return basis.T.reshape(128, 1, OWN)


def solution(mesh):
    return jax.shard_map(
        body,
        mesh=mesh,
        in_specs=(
            P("band", "dom", None),
            P(),
            P("dom"),
            P(("dom", "band"), None),
            P(("dom", "band"), None),
            P(("dom", "band")),
        ),
        out_specs=P(None, ("dom", "band"), None),
        check_vma=False,
    )
```

```python
import functools

import jax
import jax.numpy as jnp
from jax import lax
from jax.experimental import pallas as pl
from jax.experimental.pallas import tpu as pltpu
from jax.sharding import PartitionSpec as P

FACE = 81
OWN = 648
NODES = 729
WIDE = 768
HALF = 384
SLAB = 136
TILE5 = 640
SPLIT = OWN - TILE5

CENTER = -1.0
HALF_WIDTH = 2.5

X_GROUPS = [[x * 16 + r for x in range(4)] for r in range(16)]
YZ_GROUPS = [[x * 16 + r for r in range(16)] for x in range(4)]


def device(x, y, z_lo, z_hi, core):
    return ((x * 8 + y) * 2 + z_lo) * 8 + z_hi * 2 + core


NEAR_GROUPS = [[device(x, y, l, h, c) for x in range(4) for l in range(2) for c in range(2)]
               for y in range(8) for h in range(4)]
FAR_GROUPS = [[device(x, y, l, h, c) for y in range(8) for h in range(4)]
              for x in range(4) for l in range(2) for c in range(2)]


def exchange(value, axis, groups=None):
    return lax.all_to_all(value, axis, split_axis=0, concat_axis=0, tiled=True, axis_index_groups=groups)


def split2(value):
    high = value.astype(jnp.bfloat16)
    low = (value - high.astype(jnp.float32)).astype(jnp.bfloat16)
    return high, low


def dot(a, b):
    return jnp.dot(a, b, preferred_element_type=jnp.float32)


def dot_nt(a, b):
    return lax.dot_general(a, b, (((1,), (1,)), ((), ())), preferred_element_type=jnp.float32)


def pack_kernel(core_ref, owner_hbm, cell_hbm, density_hbm, scale_hbm, orbitals_hbm,
                own_ref, send_ref, left_ref, right_ref,
                owner_ref, cell_ref, density_ref, scale_ref, orbitals_ref, sems):
    copies = [
        pltpu.make_async_copy(density_hbm, density_ref, sems.at[0]),
        pltpu.make_async_copy(owner_hbm, owner_ref, sems.at[1]),
        pltpu.make_async_copy(cell_hbm, cell_ref, sems.at[2]),
        pltpu.make_async_copy(scale_hbm, scale_ref, sems.at[3]),
        pltpu.make_async_copy(orbitals_hbm, orbitals_ref, sems.at[4]),
    ]
    for copy in copies:
        copy.start()
    for copy in copies:
        copy.wait()
    for c in range(3):
        left_ref[c] = orbitals_ref[:, 5 + c, :]
        right_ref[c] = orbitals_ref[:, c, :]
    diagonal = lax.broadcasted_iota(jnp.int32, (8, 8), 0) == lax.broadcasted_iota(jnp.int32, (8, 8), 1)
    column = jnp.sum(jnp.where(diagonal, jnp.broadcast_to(scale_ref[...], (8, 8)), 0.0), 1, keepdims=True)
    for ref in (left_ref, right_ref):
        ref[3, :8, :] = jnp.broadcast_to(column, (8, OWN))
        ref[3, 8:, :] = jnp.zeros((8, OWN), jnp.float32)
    count = density_ref.shape[1]
    target = (owner_ref[...] * 8 + cell_ref[...]).astype(jnp.float32)
    target = jnp.broadcast_to(target, (8, count))

    def lower(ref):
        ref[:HALF, :] = density_ref[:HALF, :]
        ref[HALF:, :] = target

    def upper(ref):
        ref[:344, :] = density_ref[HALF:728, :]
        ref[344:HALF, :] = jnp.zeros((HALF - 344, count), jnp.float32)
        ref[344:345, :] = density_ref[728:NODES, :]
        ref[HALF:, :] = target

    @pl.when(core_ref[0] == 0)
    def _():
        lower(own_ref)
        upper(send_ref)

    @pl.when(core_ref[0] != 0)
    def _():
        upper(own_ref)
        lower(send_ref)


def deliver_kernel(own_hbm, other_hbm, out_ref, own_ref, other_ref, sems):
    copies = [
        pltpu.make_async_copy(own_hbm, own_ref, sems.at[0]),
        pltpu.make_async_copy(other_hbm, other_ref, sems.at[1]),
    ]
    for copy in copies:
        copy.start()
    rows = 4 * SLAB
    count = own_ref.shape[1]
    row = lax.broadcasted_iota(jnp.int32, (rows, count), 0)
    slab = (row >= SLAB).astype(jnp.int32) + (row >= 2 * SLAB).astype(jnp.int32) + (row >= 3 * SLAB).astype(jnp.int32)
    cell = (row - 8 * slab - 3).astype(jnp.float32)
    total = None
    for ref, copy in zip((own_ref, other_ref), copies):
        copy.wait()
        onehot = jnp.where(ref[HALF:HALF + 1, :] == cell, 1.0, 0.0).astype(jnp.bfloat16)
        values = ref[:HALF, :]
        first = values.astype(jnp.bfloat16)
        rest = values - first.astype(jnp.float32)
        second = rest.astype(jnp.bfloat16)
        third = (rest - second.astype(jnp.float32)).astype(jnp.bfloat16)
        part = dot_nt(onehot, first) + dot_nt(onehot, second) + dot_nt(onehot, third)
        total = part if total is None else total + part
    out_ref[...] = total


def window_kernel(part_ref, out_ref):
    for k in range(17):
        r = slice(8 * k, 8 * k + 8)
        block = (part_ref[0, r, :] + part_ref[1, r, :]) + (part_ref[2, r, :] + part_ref[3, r, :])
        if k < 16:
            out_ref[k, :8, :] = block
        if k > 0:
            out_ref[k - 1, 8:, :] = block


def filter_kernel(last_ref, scale_ref, own_ref, left_ref, right_ref, part_ref, operator_ref, out_ref,
                  kwide, khigh, klow, v0, v1, v2, chigh, clow, cell_buf, product, pot):
    kwide[720:, :] = jnp.zeros((WIDE - 720, WIDE), jnp.float32)
    kwide[:, TILE5:] = jnp.zeros((WIDE, WIDE - TILE5), jnp.float32)
    kwide[:NODES, :NODES] = operator_ref[...]
    for i in range(0, WIDE, 128):
        high, low = split2(kwide[i:i + 128, :])
        khigh[i:i + 128, :] = high
        klow[i:i + 128, :] = low
    for half in range(2):
        rho = (part_ref[half] + part_ref[half + 2]) + (part_ref[half + 4] + part_ref[half + 6])
        pot[:, half * HALF:(half + 1) * HALF] = jnp.where(
            rho > 0.0, -0.7386 * jnp.exp(jnp.log(jnp.where(rho > 0.0, rho, 1.0)) * (1.0 / 3.0)), 0.0)
    lane = lax.broadcasted_iota(jnp.int32, (16, 128), 1)
    is_face = lane < FACE
    is_own5 = lane < SPLIT
    zero5 = jnp.zeros((16, WIDE - TILE5), jnp.float32)

    def place(i, value):
        v0[16 * i:16 * i + 16, TILE5:] = zero5
        v0[16 * i:16 * i + 16, :OWN] = value

    for i in range(3):
        place(i, left_ref[i])
        place(11 + i, right_ref[i])
    for i in range(8):
        place(3 + i, own_ref[:, i, :])

    def scale_of(i):
        if i < 3:
            line = left_ref[3, 5 + i:6 + i, :128]
        elif i < 11:
            line = scale_ref[i - 3]
        else:
            line = right_ref[3, i - 11:i - 10, :128]
        return line

    alive = last_ref[0].astype(jnp.float32)

    def apply(source, begin, end, combine):
        for i in range(begin, end):
            r = slice(16 * i, 16 * i + 16)
            n = slice(16 * i + 16, 16 * i + 32)
            for t in range(6):
                c = slice(128 * t, 128 * t + 128)
                value = source[r, c]
                if t == 5:
                    face = jnp.where(is_face, source[n, :128], 0.0)
                    value = value + pltpu.roll(face, SPLIT, 1)
                cell_buf[r, c] = value
                high, low = split2(value)
                chigh[r, c] = high
                clow[r, c] = low
        r = slice(16 * begin, 16 * end)
        a, b = chigh[r, :], clow[r, :]
        product[r, :] = dot(a, khigh[...]) + dot(b, khigh[...]) + dot(a, klow[...])
        tail = None
        for i in range(begin, end):
            r = slice(16 * i, 16 * i + 16)
            scale = scale_of(i)
            parts = []
            for t in range(6):
                c = slice(128 * t, 128 * t + 128)
                parts.append(scale * product[r, c] + pot[i:i + 1, c] * cell_buf[r, c])
            if tail is not None:
                add = jnp.where(is_face, pltpu.roll(tail, 128 - SPLIT, 1), 0.0)
                if i == 11:
                    add = add * alive
                parts[0] = parts[0] + add
                for t in range(6):
                    value = parts[t]
                    if t == 5:
                        value = jnp.where(is_own5, value, 0.0)
                    combine(i, t, value)
            tail = parts[5]

    def at(ref, i, t):
        return ref[16 * i:16 * i + 16, 128 * t:128 * t + 128]

    def first(i, t, value):
        v1[16 * i:16 * i + 16, 128 * t:128 * t + 128] = (value - CENTER * at(v0, i, t)) * (1.0 / HALF_WIDTH)

    def second(i, t, value):
        v2[16 * i:16 * i + 16, 128 * t:128 * t + 128] = (value - CENTER * at(v1, i, t)) * (2.0 / HALF_WIDTH) - at(v0, i, t)

    def third(i, t, value):
        result = (value - CENTER * at(v2, i, t)) * (2.0 / HALF_WIDTH) - at(v1, i, t)
        if t < 5:
            out_ref[i - 3, :, 128 * t:128 * t + 128] = result
        else:
            out_ref[i - 3, :, TILE5:OWN] = result[:, :SPLIT]

    apply(v0, 0, 13, first)
    apply(v1, 1, 12, second)
    apply(v2, 2, 11, third)


def solve_kernel(total, gram_ref, flat_ref, out_ref, inverse_ref):
    shape = (8, 128)
    col = lax.broadcasted_iota(jnp.int32, shape, 1)
    row = lax.broadcasted_iota(jnp.int32, shape, 0)
    a = [gram_ref[8 * i:8 * i + 8, :] * (1.0 / total) for i in range(16)]
    w = [jnp.where(col == row + 8 * i, 1.0, 0.0) for i in range(16)]

    def columns(block, k):
        return [jnp.broadcast_to(block[:, 8 * k + j:8 * k + j + 1], shape) for j in range(8)]

    def line(block, i):
        return jnp.broadcast_to(block[i:i + 1, :], shape)

    for k in range(16):
        own = columns(a[k], k)
        s = [[line(own[j], i) for j in range(i + 1)] for i in range(8)]
        low = [[None] * 8 for _ in range(8)]
        inv = [None] * 8
        for j in range(8):
            inv[j] = 1.0 / s[j][j]
            for i in range(j + 1, 8):
                low[i][j] = s[i][j] * inv[j]
            for i in range(j + 1, 8):
                for m in range(j + 1, i + 1):
                    s[i][m] = s[i][m] - low[i][j] * s[m][j]
        n = [[None] * 8 for _ in range(8)]
        for i in range(8):
            for j in range(i):
                value = low[i][j]
                for m in range(j + 1, i):
                    value = value + low[i][m] * n[m][j]
                n[i][j] = -value

        def forward(block):
            lines = [line(block, i) for i in range(8)]
            result = []
            for i in range(8):
                value = lines[i]
                for j in range(i):
                    value = value + n[i][j] * lines[j]
                result.append(value)
            return result

        def backward(lines):
            scaled = [inv[i] * lines[i] for i in range(8)]
            result = []
            for j in range(8):
                value = scaled[j]
                for i in range(j + 1, 8):
                    value = value + n[i][j] * scaled[i]
                result.append(value)
            return result

        lines_w = forward(w[k])
        final = jnp.zeros(shape, jnp.float32)
        for i in range(8):
            final = jnp.where(row == i, lines_w[i] * jnp.sqrt(inv[i]), final)
        inverse_ref[8 * k:8 * k + 8, :] = final
        if k < 15:
            za = backward(forward(a[k]))
            zw = backward(lines_w)
            for i in range(k + 1, 16):
                c = columns(a[i], k)
                for j in range(8):
                    a[i] = a[i] - c[j] * za[j]
                    w[i] = w[i] - c[j] * zw[j]
    inverse_high, inverse_low = split2(inverse_ref[...])
    for begin in range(0, OWN, 128):
        c = slice(begin, min(begin + 128, OWN))
        flat_high, flat_low = split2(jnp.transpose(flat_ref[:, c]))
        out_ref[c, :] = (dot_nt(flat_high, inverse_high) + dot_nt(flat_low, inverse_high)
                         + dot_nt(flat_high, inverse_low))


def body(orbitals, cell_operator, cell_scale, density, block_owner, block_cell):
    dom_count = lax.axis_size("dom")
    band_count = lax.axis_size("band")
    dom = lax.axis_index("dom")
    core = jnp.reshape(lax.axis_index("band") % 2, (1,)).astype(jnp.int32)
    alive = jnp.reshape((dom < dom_count - 1).astype(jnp.int32), (1,))
    smem = pl.BlockSpec(memory_space=pltpu.SMEM)
    vmem = pl.BlockSpec(memory_space=pltpu.VMEM)
    hbm = pl.BlockSpec(memory_space=pltpu.HBM)
    params = pltpu.CompilerParams(vmem_limit_bytes=16 << 20)
    roomy = pltpu.CompilerParams(vmem_limit_bytes=62 << 20)

    count = density.shape[0]
    pack_shape = jax.ShapeDtypeStruct((HALF + 8, count), jnp.float32)
    ghost_shape = jax.ShapeDtypeStruct((4, 16, OWN), jnp.float32)
    own, send, send_left, send_right = pl.pallas_call(
        pack_kernel,
        out_shape=(pack_shape, pack_shape, ghost_shape, ghost_shape),
        in_specs=[smem] + [hbm] * 5,
        out_specs=(vmem,) * 4,
        scratch_shapes=[
            pltpu.VMEM((1, count), jnp.int32),
            pltpu.VMEM((1, count), jnp.int32),
            pltpu.VMEM((NODES, count), jnp.float32),
            pltpu.VMEM((1, 8), jnp.float32),
            pltpu.VMEM((16, 8, OWN), jnp.float32),
            pltpu.SemaphoreType.DMA((5,)),
        ],
        compiler_params=roomy,
        name="pack",
    )(core, block_owner.reshape(1, -1), block_cell.reshape(1, -1), density.T, cell_scale.reshape(1, -1), orbitals)
    other = lax.ppermute(send, "band", [(i, i ^ 1) for i in range(band_count)])
    delivered = pl.pallas_call(
        deliver_kernel,
        out_shape=jax.ShapeDtypeStruct((4 * SLAB, HALF), jnp.float32),
        in_specs=[hbm, hbm],
        out_specs=vmem,
        scratch_shapes=[
            pltpu.VMEM((HALF + 8, count), jnp.float32),
            pltpu.VMEM((HALF + 8, count), jnp.float32),
            pltpu.SemaphoreType.DMA((2,)),
        ],
        compiler_params=roomy,
        name="deliver",
    )(own, other)

    left = lax.ppermute(send_left, "dom", [(i, i + 1) for i in range(dom_count - 1)])
    right = lax.ppermute(send_right, "dom", [(i + 1, i) for i in range(dom_count - 1)])

    part = exchange(delivered.reshape(4, SLAB, HALF), "dom", X_GROUPS)
    windows = pl.pallas_call(
        window_kernel,
        out_shape=jax.ShapeDtypeStruct((16, 16, HALF), jnp.float32),
        in_specs=[vmem],
        out_specs=vmem,
        compiler_params=params,
        name="windows",
    )(part)
    windows, left, right = lax.optimization_barrier((windows, left, right))
    part = exchange(windows, "dom", YZ_GROUPS)
    window = jnp.sum(part, 0)
    part = exchange(jnp.broadcast_to(window[None], (band_count, 16, HALF)), "band")

    filtered = pl.pallas_call(
        filter_kernel,
        out_shape=jax.ShapeDtypeStruct((8, 16, OWN), jnp.float32),
        in_specs=[smem] * 2 + [vmem] * 5,
        out_specs=vmem,
        scratch_shapes=[
            pltpu.VMEM((WIDE, WIDE), jnp.float32),
            pltpu.VMEM((WIDE, WIDE), jnp.bfloat16),
            pltpu.VMEM((WIDE, WIDE), jnp.bfloat16),
            pltpu.VMEM((224, WIDE), jnp.float32),
            pltpu.VMEM((224, WIDE), jnp.float32),
            pltpu.VMEM((224, WIDE), jnp.float32),
            pltpu.VMEM((224, WIDE), jnp.bfloat16),
            pltpu.VMEM((224, WIDE), jnp.bfloat16),
            pltpu.VMEM((224, WIDE), jnp.float32),
            pltpu.VMEM((224, WIDE), jnp.float32),
            pltpu.VMEM((16, WIDE), jnp.float32),
        ],
        compiler_params=params,
        name="chebyshev",
    )(alive, cell_scale, orbitals, left, right, part, cell_operator)

    flat = exchange(filtered, "band").reshape(128, OWN)
    both = ("dom", "band")
    total = OWN * dom_count * band_count
    gram = jnp.dot(flat, flat.T, precision=lax.Precision.HIGHEST)
    part = jnp.sum(exchange(gram.reshape(16, 8, 128), both, NEAR_GROUPS), 0)
    part = jnp.sum(exchange(jnp.broadcast_to(part[None], (32, 8, 128)), both, FAR_GROUPS), 0)
    gram = exchange(jnp.broadcast_to(part[None], (16, 8, 128)), both, NEAR_GROUPS).reshape(128, 128)
    basis = pl.pallas_call(
        functools.partial(solve_kernel, float(total)),
        out_shape=jax.ShapeDtypeStruct((OWN, 128), jnp.float32),
        in_specs=[vmem, vmem],
        out_specs=vmem,
        scratch_shapes=[pltpu.VMEM((128, 128), jnp.float32)],
        compiler_params=params,
        name="orthonormalize",
    )(gram, flat)
    return basis.T.reshape(128, 1, OWN)


def solution(mesh):
    return jax.shard_map(
        body,
        mesh=mesh,
        in_specs=(
            P("band", "dom", None),
            P(),
            P("dom"),
            P(("dom", "band"), None),
            P(("dom", "band"), None),
            P(("dom", "band")),
        ),
        out_specs=P(None, ("dom", "band"), None),
        check_vma=False,
    )
```

```python
import functools

import jax
import jax.numpy as jnp
from jax import lax
from jax.experimental import pallas as pl
from jax.experimental.pallas import tpu as pltpu
from jax.sharding import PartitionSpec as P

FACE = 81
OWN = 648
NODES = 729
WIDE = 768
HALF = 384
SLAB = 136
TILE5 = 640
SPLIT = OWN - TILE5

CENTER = -1.0
HALF_WIDTH = 2.5

X_GROUPS = [[x * 16 + r for x in range(4)] for r in range(16)]
YZ_GROUPS = [[x * 16 + r for r in range(16)] for x in range(4)]


def device(x, y, z_lo, z_hi, core):
    return ((x * 8 + y) * 2 + z_lo) * 8 + z_hi * 2 + core


NEAR_GROUPS = [[device(x, y, l, h, c) for x in range(4) for l in range(2) for c in range(2)]
               for y in range(8) for h in range(4)]
FAR_GROUPS = [[device(x, y, l, h, c) for y in range(8) for h in range(4)]
              for x in range(4) for l in range(2) for c in range(2)]


def exchange(value, axis, groups=None):
    return lax.all_to_all(value, axis, split_axis=0, concat_axis=0, tiled=True, axis_index_groups=groups)


def split2(value):
    high = value.astype(jnp.bfloat16)
    low = (value - high.astype(jnp.float32)).astype(jnp.bfloat16)
    return high, low


def dot(a, b):
    return jnp.dot(a, b, preferred_element_type=jnp.float32)


def dot_nt(a, b):
    return lax.dot_general(a, b, (((1,), (1,)), ((), ())), preferred_element_type=jnp.float32)


def pack_kernel(core_ref, owner_hbm, cell_hbm, density_hbm, scale_hbm, orbitals_hbm,
                own_ref, send_ref, left_ref, right_ref,
                owner_ref, cell_ref, density_ref, scale_ref, orbitals_ref, sems):
    copies = [
        pltpu.make_async_copy(density_hbm, density_ref, sems.at[0]),
        pltpu.make_async_copy(owner_hbm, owner_ref, sems.at[1]),
        pltpu.make_async_copy(cell_hbm, cell_ref, sems.at[2]),
        pltpu.make_async_copy(scale_hbm, scale_ref, sems.at[3]),
        pltpu.make_async_copy(orbitals_hbm, orbitals_ref, sems.at[4]),
    ]
    for copy in copies:
        copy.start()
    for copy in copies:
        copy.wait()
    def ghost(ref, place, c):
        value = orbitals_ref[:, c, :]
        scale = jnp.broadcast_to(scale_ref[:, c:c + 1], (16, 128 - SPLIT))
        ref[:, WIDE * place:WIDE * place + TILE5] = value[:, :TILE5]
        ref[:, WIDE * place + TILE5:WIDE * place + WIDE] = jnp.concatenate([value[:, TILE5:], scale], 1)

    for place in range(3):
        ghost(left_ref, place, 5 + place)
    for place in range(2):
        ghost(right_ref, place, place)
    right_ref[:, 2 * WIDE:] = orbitals_ref[:, 2, :128]
    count = density_ref.shape[1]
    target = (owner_ref[...] * 8 + cell_ref[...]).astype(jnp.float32)
    target = jnp.broadcast_to(target, (8, count))

    def lower(ref):
        ref[:HALF, :] = density_ref[:HALF, :]
        ref[HALF:, :] = target

    def upper(ref):
        ref[:344, :] = density_ref[HALF:728, :]
        ref[344:HALF, :] = jnp.zeros((HALF - 344, count), jnp.float32)
        ref[344:345, :] = density_ref[728:NODES, :]
        ref[HALF:, :] = target

    @pl.when(core_ref[0] == 0)
    def _():
        lower(own_ref)
        upper(send_ref)

    @pl.when(core_ref[0] != 0)
    def _():
        upper(own_ref)
        lower(send_ref)


def cell_sums(ref):
    rows = 4 * SLAB
    row = lax.broadcasted_iota(jnp.int32, (rows, ref.shape[1]), 0)
    slab = (row >= SLAB).astype(jnp.int32) + (row >= 2 * SLAB).astype(jnp.int32) + (row >= 3 * SLAB).astype(jnp.int32)
    cell = (row - 8 * slab - 3).astype(jnp.float32)
    onehot = jnp.where(ref[HALF:HALF + 1, :] == cell, 1.0, 0.0).astype(jnp.bfloat16)
    high, low = split2(ref[:HALF, :])
    return dot_nt(onehot, high) + dot_nt(onehot, low)


def own_kernel(own_ref, out_ref):
    out_ref[...] = cell_sums(own_ref)


def deliver_kernel(own_ref, other_ref, out_ref):
    out_ref[...] = own_ref[...] + cell_sums(other_ref)


def window_kernel(part_ref, out_ref):
    for k in range(17):
        r = slice(8 * k, 8 * k + 8)
        block = (part_ref[0, r, :] + part_ref[1, r, :]) + (part_ref[2, r, :] + part_ref[3, r, :])
        if k < 16:
            out_ref[k, :8, :] = block
        if k > 0:
            out_ref[k - 1, 8:, :] = block


def cell_vectors(source, begin, end, cell_buf, chigh, clow):
    is_face = lax.broadcasted_iota(jnp.int32, (16, 128), 1) < FACE
    for i in range(begin, end):
        r = slice(16 * i, 16 * i + 16)
        n = slice(16 * i + 16, 16 * i + 32)
        for t in range(6):
            c = slice(128 * t, 128 * t + 128)
            value = source[r, c]
            if t == 5:
                face = jnp.where(is_face, source[n, :128], 0.0)
                value = value + pltpu.roll(face, SPLIT, 1)
            cell_buf[r, c] = value
            high, low = split2(value)
            chigh[r, c] = high
            clow[r, c] = low


def products(begin, end, product, chigh, clow, ksplit):
    r = slice(16 * begin, 16 * end)
    a, b = chigh[r, :], clow[r, :]
    khigh, klow = ksplit[:WIDE, :], ksplit[WIDE:, :]
    product[r, :] = dot(a, khigh) + dot(b, khigh) + dot(a, klow)


def first_vectors(own_ref, left_ref, right_ref, v0, cell_buf, chigh, clow):
    zero5 = jnp.zeros((16, WIDE - TILE5), jnp.float32)

    def place(i, value):
        v0[16 * i:16 * i + 16, TILE5:] = zero5
        v0[16 * i:16 * i + 16, :OWN] = value

    own_lane = lax.broadcasted_iota(jnp.int32, (16, 128), 1) < SPLIT

    def ghost(i, ref, begin):
        v0[16 * i:16 * i + 16, :TILE5] = ref[:, begin:begin + TILE5]
        v0[16 * i:16 * i + 16, TILE5:] = jnp.where(own_lane, ref[:, begin + TILE5:begin + WIDE], 0.0)

    for i in range(3):
        ghost(i, left_ref, WIDE * i)
    for i in range(2):
        ghost(11 + i, right_ref, WIDE * i)
    v0[16 * 13:, :128] = right_ref[:, 2 * WIDE:]
    for i in range(8):
        place(3 + i, own_ref[:, i, :])
    cell_vectors(v0, 0, 13, cell_buf, chigh, clow)


def split_kernel(operator_ref, ksplit, kwide):
    kwide[720:, :] = jnp.zeros((WIDE - 720, WIDE), jnp.float32)
    kwide[:, TILE5:] = jnp.zeros((WIDE, WIDE - TILE5), jnp.float32)
    kwide[:NODES, :NODES] = operator_ref[...]
    for i in range(0, WIDE, 128):
        high, low = split2(kwide[i:i + 128, :])
        ksplit[i:i + 128, :] = high
        ksplit[WIDE + i:WIDE + i + 128, :] = low


def filter_kernel(last_ref, scale_ref, own_ref, left_ref, right_ref, part_ref, ksplit, out_ref,
                  v0, v1, v2, chigh, clow, cell_buf, product, pot):
    for half in range(2):
        rho = (part_ref[half] + part_ref[half + 2]) + (part_ref[half + 4] + part_ref[half + 6])
        pot[:, half * HALF:(half + 1) * HALF] = jnp.where(
            rho > 0.0, -0.7386 * jnp.exp(jnp.log(jnp.where(rho > 0.0, rho, 1.0)) * (1.0 / 3.0)), 0.0)
    lane = lax.broadcasted_iota(jnp.int32, (16, 128), 1)
    is_face = lane < FACE
    is_own5 = lane < SPLIT

    def scale_of(i):
        if i < 3:
            line = left_ref[:, WIDE * i + OWN:WIDE * i + OWN + 1]
        elif i < 11:
            line = scale_ref[i - 3]
        else:
            line = right_ref[:, WIDE * (i - 11) + OWN:WIDE * (i - 11) + OWN + 1]
        return line

    alive = last_ref[0].astype(jnp.float32)

    def assemble(begin, end, product, cells, combine):
        tail = None
        for i in range(begin, end):
            r = slice(16 * i, 16 * i + 16)
            scale = scale_of(i)
            parts = []
            for t in range(6):
                c = slice(128 * t, 128 * t + 128)
                parts.append(scale * product[r, c] + pot[i:i + 1, c] * cells[r, c])
            if tail is not None:
                add = jnp.where(is_face, pltpu.roll(tail, 128 - SPLIT, 1), 0.0)
                if i == 11:
                    add = add * alive
                parts[0] = parts[0] + add
                for t in range(6):
                    value = parts[t]
                    if t == 5:
                        value = jnp.where(is_own5, value, 0.0)
                    combine(i, t, value)
            tail = parts[5]

    def apply(source, begin, end, combine):
        cell_vectors(source, begin, end, cell_buf, chigh, clow)
        products(begin, end, product, chigh, clow, ksplit)
        assemble(begin, end, product, cell_buf, combine)

    def at(ref, i, t):
        return ref[16 * i:16 * i + 16, 128 * t:128 * t + 128]

    def first(i, t, value):
        v1[16 * i:16 * i + 16, 128 * t:128 * t + 128] = (value - CENTER * at(v0, i, t)) * (1.0 / HALF_WIDTH)

    def second(i, t, value):
        v2[16 * i:16 * i + 16, 128 * t:128 * t + 128] = (value - CENTER * at(v1, i, t)) * (2.0 / HALF_WIDTH) - at(v0, i, t)

    def third(i, t, value):
        result = (value - CENTER * at(v2, i, t)) * (2.0 / HALF_WIDTH) - at(v1, i, t)
        if t < 5:
            out_ref[i - 3, :, 128 * t:128 * t + 128] = result
        else:
            out_ref[i - 3, :, TILE5:OWN] = result[:, :SPLIT]

    first_vectors(own_ref, left_ref, right_ref, v0, cell_buf, chigh, clow)
    products(0, 13, product, chigh, clow, ksplit)
    assemble(0, 13, product, cell_buf, first)
    apply(v1, 1, 12, second)
    apply(v2, 2, 11, third)


def solve_kernel(total, gram_ref, flat_ref, out_ref, inverse_ref):
    shape = (8, 128)
    col = lax.broadcasted_iota(jnp.int32, shape, 1)
    row = lax.broadcasted_iota(jnp.int32, shape, 0)
    a = [gram_ref[8 * i:8 * i + 8, :] * (1.0 / total) for i in range(16)]
    w = [jnp.where(col == row + 8 * i, 1.0, 0.0) for i in range(16)]

    def columns(block, k):
        return [jnp.broadcast_to(block[:, 8 * k + j:8 * k + j + 1], shape) for j in range(8)]

    def line(block, i):
        return jnp.broadcast_to(block[i:i + 1, :], shape)

    for k in range(16):
        own = columns(a[k], k)
        s = [[line(own[j], i) for j in range(i + 1)] for i in range(8)]
        low = [[None] * 8 for _ in range(8)]
        inv = [None] * 8
        for j in range(8):
            inv[j] = 1.0 / s[j][j]
            for i in range(j + 1, 8):
                low[i][j] = s[i][j] * inv[j]
            for i in range(j + 1, 8):
                for m in range(j + 1, i + 1):
                    s[i][m] = s[i][m] - low[i][j] * s[m][j]
        n = [[None] * 8 for _ in range(8)]
        for i in range(8):
            for j in range(i):
                value = low[i][j]
                for m in range(j + 1, i):
                    value = value + low[i][m] * n[m][j]
                n[i][j] = -value

        def forward(block):
            lines = [line(block, i) for i in range(8)]
            result = []
            for i in range(8):
                value = lines[i]
                for j in range(i):
                    value = value + n[i][j] * lines[j]
                result.append(value)
            return result

        def backward(lines):
            scaled = [inv[i] * lines[i] for i in range(8)]
            result = []
            for j in range(8):
                value = scaled[j]
                for i in range(j + 1, 8):
                    value = value + n[i][j] * scaled[i]
                result.append(value)
            return result

        lines_w = forward(w[k])
        final = jnp.zeros(shape, jnp.float32)
        for i in range(8):
            final = jnp.where(row == i, lines_w[i] * jnp.sqrt(inv[i]), final)
        inverse_ref[8 * k:8 * k + 8, :] = final
        if k < 15:
            za = backward(forward(a[k]))
            zw = backward(lines_w)
            for i in range(k + 1, 16):
                c = columns(a[i], k)
                for j in range(8):
                    a[i] = a[i] - c[j] * za[j]
                    w[i] = w[i] - c[j] * zw[j]
    inverse_high, inverse_low = split2(inverse_ref[...])
    for begin in range(0, OWN, 128):
        c = slice(begin, min(begin + 128, OWN))
        flat_high, flat_low = split2(jnp.transpose(flat_ref[:, c]))
        out_ref[c, :] = (dot_nt(flat_high, inverse_high) + dot_nt(flat_low, inverse_high)
                         + dot_nt(flat_high, inverse_low))


def body(orbitals, cell_operator, cell_scale, density, block_owner, block_cell):
    dom_count = lax.axis_size("dom")
    band_count = lax.axis_size("band")
    dom = lax.axis_index("dom")
    core = jnp.reshape(lax.axis_index("band") % 2, (1,)).astype(jnp.int32)
    alive = jnp.reshape((dom < dom_count - 1).astype(jnp.int32), (1,))
    smem = pl.BlockSpec(memory_space=pltpu.SMEM)
    vmem = pl.BlockSpec(memory_space=pltpu.VMEM)
    hbm = pl.BlockSpec(memory_space=pltpu.HBM)
    params = pltpu.CompilerParams(vmem_limit_bytes=16 << 20)
    roomy = pltpu.CompilerParams(vmem_limit_bytes=62 << 20)

    count = density.shape[0]
    pack_shape = jax.ShapeDtypeStruct((HALF + 8, count), jnp.float32)
    left_shape = jax.ShapeDtypeStruct((16, 3 * WIDE), jnp.float32)
    right_shape = jax.ShapeDtypeStruct((16, 2 * WIDE + 128), jnp.float32)
    own, send, send_left, send_right = pl.pallas_call(
        pack_kernel,
        out_shape=(pack_shape, pack_shape, left_shape, right_shape),
        in_specs=[smem] + [hbm] * 5,
        out_specs=(vmem,) * 4,
        scratch_shapes=[
            pltpu.VMEM((1, count), jnp.int32),
            pltpu.VMEM((1, count), jnp.int32),
            pltpu.VMEM((NODES, count), jnp.float32),
            pltpu.VMEM((1, 8), jnp.float32),
            pltpu.VMEM((16, 8, OWN), jnp.float32),
            pltpu.SemaphoreType.DMA((5,)),
        ],
        compiler_params=roomy,
        name="pack",
    )(core, block_owner.reshape(1, -1), block_cell.reshape(1, -1), density.T, cell_scale.reshape(1, -1), orbitals)
    other = lax.ppermute(send, "band", [(i, i ^ 1) for i in range(band_count)])
    own = pl.pallas_call(
        own_kernel,
        out_shape=jax.ShapeDtypeStruct((4 * SLAB, HALF), jnp.float32),
        in_specs=[vmem],
        out_specs=vmem,
        compiler_params=params,
        name="own_sums",
    )(own)
    delivered = pl.pallas_call(
        deliver_kernel,
        out_shape=jax.ShapeDtypeStruct((4 * SLAB, HALF), jnp.float32),
        in_specs=[vmem, vmem],
        out_specs=vmem,
        compiler_params=params,
        name="deliver",
    )(own, other)

    left = lax.ppermute(send_left, "dom", [(i, i + 1) for i in range(dom_count - 1)])
    right = lax.ppermute(send_right, "dom", [(i + 1, i) for i in range(dom_count - 1)])

    part = exchange(delivered.reshape(4, SLAB, HALF), "dom", X_GROUPS)
    windows = pl.pallas_call(
        window_kernel,
        out_shape=jax.ShapeDtypeStruct((16, 16, HALF), jnp.float32),
        in_specs=[vmem],
        out_specs=vmem,
        compiler_params=params,
        name="windows",
    )(part)
    windows, left, right = lax.optimization_barrier((windows, left, right))
    part = exchange(windows, "dom", YZ_GROUPS)
    window = jnp.sum(part, 0)
    window, operator = lax.optimization_barrier((window, cell_operator))
    part = exchange(jnp.broadcast_to(window[None], (band_count, 16, HALF)), "band")

    ksplit = pl.pallas_call(
        split_kernel,
        out_shape=jax.ShapeDtypeStruct((2 * WIDE, WIDE), jnp.bfloat16),
        in_specs=[vmem],
        out_specs=vmem,
        scratch_shapes=[pltpu.VMEM((WIDE, WIDE), jnp.float32)],
        compiler_params=params,
        name="split_operator",
    )(operator)
    filtered = pl.pallas_call(
        filter_kernel,
        out_shape=jax.ShapeDtypeStruct((8, 16, OWN), jnp.float32),
        in_specs=[smem] * 2 + [vmem] * 5,
        out_specs=vmem,
        scratch_shapes=[
            pltpu.VMEM((224, WIDE), jnp.float32),
            pltpu.VMEM((224, WIDE), jnp.float32),
            pltpu.VMEM((224, WIDE), jnp.float32),
            pltpu.VMEM((224, WIDE), jnp.bfloat16),
            pltpu.VMEM((224, WIDE), jnp.bfloat16),
            pltpu.VMEM((224, WIDE), jnp.float32),
            pltpu.VMEM((224, WIDE), jnp.float32),
            pltpu.VMEM((16, WIDE), jnp.float32),
        ],
        compiler_params=params,
        name="chebyshev",
    )(alive, cell_scale, orbitals, left, right, part, ksplit)

    flat = exchange(filtered, "band").reshape(128, OWN)
    both = ("dom", "band")
    total = OWN * dom_count * band_count
    gram = jnp.dot(flat, flat.T, precision=lax.Precision.HIGHEST)
    part = jnp.sum(exchange(gram.reshape(16, 8, 128), both, NEAR_GROUPS), 0)
    part = jnp.sum(exchange(jnp.broadcast_to(part[None], (32, 8, 128)), both, FAR_GROUPS), 0)
    gram = exchange(jnp.broadcast_to(part[None], (16, 8, 128)), both, NEAR_GROUPS).reshape(128, 128)
    basis = pl.pallas_call(
        functools.partial(solve_kernel, float(total)),
        out_shape=jax.ShapeDtypeStruct((OWN, 128), jnp.float32),
        in_specs=[vmem, vmem],
        out_specs=vmem,
        scratch_shapes=[pltpu.VMEM((128, 128), jnp.float32)],
        compiler_params=params,
        name="orthonormalize",
    )(gram, flat)
    return basis.T.reshape(128, 1, OWN)


def solution(mesh):
    return jax.shard_map(
        body,
        mesh=mesh,
        in_specs=(
            P("band", "dom", None),
            P(),
            P("dom"),
            P(("dom", "band"), None),
            P(("dom", "band"), None),
            P(("dom", "band")),
        ),
        out_specs=P(None, ("dom", "band"), None),
        check_vma=False,
    )
```

```python
import functools

import jax
import jax.numpy as jnp
from jax import lax
from jax.experimental import pallas as pl
from jax.experimental.pallas import tpu as pltpu
from jax.sharding import PartitionSpec as P

FACE = 81
OWN = 648
NODES = 729
WIDE = 768
HALF = 384
SLAB = 136
KEPT = 13
PACKED = 40
TILE5 = 640
SPLIT = OWN - TILE5

CENTER = -1.0
HALF_WIDTH = 2.5

X_GROUPS = [[x * 16 + r for x in range(4)] for r in range(16)]
YZ_GROUPS = [[x * 16 + r for r in range(16)] for x in range(4)]


def device(x, y, z_lo, z_hi, core):
    return ((x * 8 + y) * 2 + z_lo) * 8 + z_hi * 2 + core


NEAR_GROUPS = [[device(x, y, l, h, c) for x in range(4) for l in range(2) for c in range(2)]
               for y in range(8) for h in range(4)]
FAR_GROUPS = [[device(x, y, l, h, c) for y in range(8) for h in range(4)]
              for x in range(4) for l in range(2) for c in range(2)]


def exchange(value, axis, groups=None):
    return lax.all_to_all(value, axis, split_axis=0, concat_axis=0, tiled=True, axis_index_groups=groups)


def split2(value):
    high = value.astype(jnp.bfloat16)
    low = (value - high.astype(jnp.float32)).astype(jnp.bfloat16)
    return high, low


def dot(a, b):
    return jnp.dot(a, b, preferred_element_type=jnp.float32)


def dot_nt(a, b):
    return lax.dot_general(a, b, (((1,), (1,)), ((), ())), preferred_element_type=jnp.float32)


def pack_kernel(core_ref, owner_hbm, cell_hbm, density_hbm, scale_hbm, orbitals_hbm,
                own_ref, send_ref, left_ref, right_ref,
                owner_ref, cell_ref, density_ref, scale_ref, orbitals_ref, sems):
    copies = [
        pltpu.make_async_copy(density_hbm, density_ref, sems.at[0]),
        pltpu.make_async_copy(owner_hbm, owner_ref, sems.at[1]),
        pltpu.make_async_copy(cell_hbm, cell_ref, sems.at[2]),
        pltpu.make_async_copy(scale_hbm, scale_ref, sems.at[3]),
        pltpu.make_async_copy(orbitals_hbm, orbitals_ref, sems.at[4]),
    ]
    for copy in copies:
        copy.start()
    for copy in copies[:3]:
        copy.wait()

    def ghost(ref, place, c):
        value = orbitals_ref[:, c, :]
        scale = jnp.broadcast_to(scale_ref[:, c:c + 1], (16, 128 - SPLIT))
        ref[:, WIDE * place:WIDE * place + TILE5] = value[:, :TILE5]
        ref[:, WIDE * place + TILE5:WIDE * place + WIDE] = jnp.concatenate([value[:, TILE5:], scale], 1)

    count = density_ref.shape[1]
    target = (owner_ref[...] * 8 + cell_ref[...]).astype(jnp.float32)
    target = jnp.broadcast_to(target, (8, count))

    def lower(ref):
        ref[:HALF, :] = density_ref[:HALF, :]
        ref[HALF:, :] = target

    def upper(ref):
        ref[:344, :] = density_ref[HALF:728, :]
        ref[344:HALF, :] = jnp.zeros((HALF - 344, count), jnp.float32)
        ref[344:345, :] = density_ref[728:NODES, :]
        ref[HALF:, :] = target

    @pl.when(core_ref[0] == 0)
    def _():
        lower(own_ref)
        upper(send_ref)

    @pl.when(core_ref[0] != 0)
    def _():
        upper(own_ref)
        lower(send_ref)

    for copy in copies[3:]:
        copy.wait()
    for place in range(3):
        ghost(left_ref, place, 5 + place)
    for place in range(2):
        ghost(right_ref, place, place)
    right_ref[:, 2 * WIDE:] = orbitals_ref[:, 2, :128]


def cell_sums(ref):
    rows = 4 * SLAB
    row = lax.broadcasted_iota(jnp.int32, (rows, ref.shape[1]), 0)
    slab = (row >= SLAB).astype(jnp.int32) + (row >= 2 * SLAB).astype(jnp.int32) + (row >= 3 * SLAB).astype(jnp.int32)
    cell = (row - 8 * slab - 3).astype(jnp.float32)
    onehot = jnp.where(ref[HALF:HALF + 1, :] == cell, 1.0, 0.0).astype(jnp.bfloat16)
    high, low = split2(ref[:HALF, :])
    return dot_nt(onehot, high) + dot_nt(onehot, low)


def own_kernel(own_ref, out_ref):
    out_ref[...] = cell_sums(own_ref)


def deliver_kernel(own_ref, other_ref, out_ref):
    out_ref[...] = own_ref[...] + cell_sums(other_ref)


def window_kernel(part_ref, out_ref, sum_ref):
    sum_ref[...] = (part_ref[0] + part_ref[1]) + (part_ref[2] + part_ref[3])
    for k in range(16):
        for t in range(3):
            out_ref[k, KEPT * t:KEPT * t + KEPT, :] = sum_ref[8 * k:8 * k + KEPT, 128 * t:128 * t + 128]
        out_ref[k, 3 * KEPT:, :] = jnp.zeros((PACKED - 3 * KEPT, 128), jnp.float32)


def cell_vectors(source, begin, end, cell_buf, chigh, clow):
    is_face = lax.broadcasted_iota(jnp.int32, (16, 128), 1) < FACE
    for i in range(begin, end):
        r = slice(16 * i, 16 * i + 16)
        n = slice(16 * i + 16, 16 * i + 32)
        for t in range(6):
            c = slice(128 * t, 128 * t + 128)
            value = source[r, c]
            if t == 5:
                face = jnp.where(is_face, source[n, :128], 0.0)
                value = value + pltpu.roll(face, SPLIT, 1)
            cell_buf[r, c] = value
            high, low = split2(value)
            chigh[r, c] = high
            clow[r, c] = low


def products(begin, end, product, chigh, clow, ksplit):
    r = slice(16 * begin, 16 * end)
    a, b = chigh[r, :], clow[r, :]
    khigh, klow = ksplit[:WIDE, :], ksplit[WIDE:, :]
    product[r, :] = dot(a, khigh) + dot(b, khigh) + dot(a, klow)


def first_vectors(own_ref, left_ref, right_ref, v0, cell_buf, chigh, clow):
    zero5 = jnp.zeros((16, WIDE - TILE5), jnp.float32)

    def place(i, value):
        v0[16 * i:16 * i + 16, TILE5:] = zero5
        v0[16 * i:16 * i + 16, :OWN] = value

    own_lane = lax.broadcasted_iota(jnp.int32, (16, 128), 1) < SPLIT

    def ghost(i, ref, begin):
        v0[16 * i:16 * i + 16, :TILE5] = ref[:, begin:begin + TILE5]
        v0[16 * i:16 * i + 16, TILE5:] = jnp.where(own_lane, ref[:, begin + TILE5:begin + WIDE], 0.0)

    for i in range(3):
        ghost(i, left_ref, WIDE * i)
    for i in range(2):
        ghost(11 + i, right_ref, WIDE * i)
    v0[16 * 13:, :128] = right_ref[:, 2 * WIDE:]
    for i in range(8):
        place(3 + i, own_ref[:, i, :])
    cell_vectors(v0, 0, 13, cell_buf, chigh, clow)


def split_kernel(operator_ref, ksplit, kwide):
    kwide[720:, :] = jnp.zeros((WIDE - 720, WIDE), jnp.float32)
    kwide[:, TILE5:] = jnp.zeros((WIDE, WIDE - TILE5), jnp.float32)
    kwide[:NODES, :NODES] = operator_ref[...]
    for i in range(0, WIDE, 128):
        high, low = split2(kwide[i:i + 128, :])
        ksplit[i:i + 128, :] = high
        ksplit[WIDE + i:WIDE + i + 128, :] = low


def filter_kernel(last_ref, scale_ref, own_ref, left_ref, right_ref, part_ref, ksplit, out_ref,
                  v0, v1, v2, chigh, clow, cell_buf, product, pot):
    for half in range(2):
        rho = (part_ref[half] + part_ref[half + 2]) + (part_ref[half + 4] + part_ref[half + 6])
        value = jnp.where(
            rho > 0.0, -0.7386 * jnp.exp(jnp.log(jnp.where(rho > 0.0, rho, 1.0)) * (1.0 / 3.0)), 0.0)
        for t in range(3):
            begin = half * HALF + 128 * t
            pot[:KEPT, begin:begin + 128] = value[KEPT * t:KEPT * t + KEPT, :]
    lane = lax.broadcasted_iota(jnp.int32, (16, 128), 1)
    is_face = lane < FACE
    is_own5 = lane < SPLIT

    def scale_of(i):
        if i < 3:
            line = left_ref[:, WIDE * i + OWN:WIDE * i + OWN + 1]
        elif i < 11:
            line = scale_ref[i - 3]
        else:
            line = right_ref[:, WIDE * (i - 11) + OWN:WIDE * (i - 11) + OWN + 1]
        return line

    alive = last_ref[0].astype(jnp.float32)

    def assemble(begin, end, product, cells, combine):
        tail = None
        for i in range(begin, end):
            r = slice(16 * i, 16 * i + 16)
            scale = scale_of(i)
            parts = []
            for t in range(6):
                c = slice(128 * t, 128 * t + 128)
                parts.append(scale * product[r, c] + pot[i:i + 1, c] * cells[r, c])
            if tail is not None:
                add = jnp.where(is_face, pltpu.roll(tail, 128 - SPLIT, 1), 0.0)
                if i == 11:
                    add = add * alive
                parts[0] = parts[0] + add
                for t in range(6):
                    value = parts[t]
                    if t == 5:
                        value = jnp.where(is_own5, value, 0.0)
                    combine(i, t, value)
            tail = parts[5]

    def apply(source, begin, end, combine):
        cell_vectors(source, begin, end, cell_buf, chigh, clow)
        products(begin, end, product, chigh, clow, ksplit)
        assemble(begin, end, product, cell_buf, combine)

    def at(ref, i, t):
        return ref[16 * i:16 * i + 16, 128 * t:128 * t + 128]

    def first(i, t, value):
        v1[16 * i:16 * i + 16, 128 * t:128 * t + 128] = (value - CENTER * at(v0, i, t)) * (1.0 / HALF_WIDTH)

    def second(i, t, value):
        v2[16 * i:16 * i + 16, 128 * t:128 * t + 128] = (value - CENTER * at(v1, i, t)) * (2.0 / HALF_WIDTH) - at(v0, i, t)

    def third(i, t, value):
        result = (value - CENTER * at(v2, i, t)) * (2.0 / HALF_WIDTH) - at(v1, i, t)
        if t < 5:
            out_ref[i - 3, :, 128 * t:128 * t + 128] = result
        else:
            out_ref[i - 3, :, TILE5:OWN] = result[:, :SPLIT]

    first_vectors(own_ref, left_ref, right_ref, v0, cell_buf, chigh, clow)
    products(0, 13, product, chigh, clow, ksplit)
    assemble(0, 13, product, cell_buf, first)
    apply(v1, 1, 12, second)
    apply(v2, 2, 11, third)


def solve_kernel(total, gram_ref, flat_ref, out_ref, inverse_ref):
    shape = (8, 128)
    col = lax.broadcasted_iota(jnp.int32, shape, 1)
    row = lax.broadcasted_iota(jnp.int32, shape, 0)
    a = [gram_ref[8 * i:8 * i + 8, :] * (1.0 / total) for i in range(16)]
    w = [jnp.where(col == row + 8 * i, 1.0, 0.0) for i in range(16)]

    def columns(block, k):
        return [jnp.broadcast_to(block[:, 8 * k + j:8 * k + j + 1], shape) for j in range(8)]

    def line(block, i):
        return jnp.broadcast_to(block[i:i + 1, :], shape)

    for k in range(16):
        own = columns(a[k], k)
        s = [[line(own[j], i) for j in range(i + 1)] for i in range(8)]
        low = [[None] * 8 for _ in range(8)]
        inv = [None] * 8
        for j in range(8):
            inv[j] = 1.0 / s[j][j]
            for i in range(j + 1, 8):
                low[i][j] = s[i][j] * inv[j]
            for i in range(j + 1, 8):
                for m in range(j + 1, i + 1):
                    s[i][m] = s[i][m] - low[i][j] * s[m][j]
        n = [[None] * 8 for _ in range(8)]
        for i in range(8):
            for j in range(i):
                value = low[i][j]
                for m in range(j + 1, i):
                    value = value + low[i][m] * n[m][j]
                n[i][j] = -value

        def forward(block):
            lines = [line(block, i) for i in range(8)]
            result = []
            for i in range(8):
                value = lines[i]
                for j in range(i):
                    value = value + n[i][j] * lines[j]
                result.append(value)
            return result

        def backward(lines):
            scaled = [inv[i] * lines[i] for i in range(8)]
            result = []
            for j in range(8):
                value = scaled[j]
                for i in range(j + 1, 8):
                    value = value + n[i][j] * scaled[i]
                result.append(value)
            return result

        lines_w = forward(w[k])
        final = jnp.zeros(shape, jnp.float32)
        for i in range(8):
            final = jnp.where(row == i, lines_w[i] * jnp.sqrt(inv[i]), final)
        inverse_ref[8 * k:8 * k + 8, :] = final
        if k < 15:
            za = backward(forward(a[k]))
            zw = backward(lines_w)
            for i in range(k + 1, 16):
                c = columns(a[i], k)
                for j in range(8):
                    a[i] = a[i] - c[j] * za[j]
                    w[i] = w[i] - c[j] * zw[j]
    inverse_high, inverse_low = split2(inverse_ref[...])
    for begin in range(0, OWN, 128):
        c = slice(begin, min(begin + 128, OWN))
        flat_high, flat_low = split2(jnp.transpose(flat_ref[:, c]))
        out_ref[c, :] = (dot_nt(flat_high, inverse_high) + dot_nt(flat_low, inverse_high)
                         + dot_nt(flat_high, inverse_low))


def body(orbitals, cell_operator, cell_scale, density, block_owner, block_cell):
    dom_count = lax.axis_size("dom")
    band_count = lax.axis_size("band")
    dom = lax.axis_index("dom")
    core = jnp.reshape(lax.axis_index("band") % 2, (1,)).astype(jnp.int32)
    alive = jnp.reshape((dom < dom_count - 1).astype(jnp.int32), (1,))
    smem = pl.BlockSpec(memory_space=pltpu.SMEM)
    vmem = pl.BlockSpec(memory_space=pltpu.VMEM)
    hbm = pl.BlockSpec(memory_space=pltpu.HBM)
    params = pltpu.CompilerParams(vmem_limit_bytes=16 << 20)
    roomy = pltpu.CompilerParams(vmem_limit_bytes=62 << 20)

    count = density.shape[0]
    pack_shape = jax.ShapeDtypeStruct((HALF + 8, count), jnp.float32)
    left_shape = jax.ShapeDtypeStruct((16, 3 * WIDE), jnp.float32)
    right_shape = jax.ShapeDtypeStruct((16, 2 * WIDE + 128), jnp.float32)
    own, send, send_left, send_right = pl.pallas_call(
        pack_kernel,
        out_shape=(pack_shape, pack_shape, left_shape, right_shape),
        in_specs=[smem] + [hbm] * 5,
        out_specs=(vmem,) * 4,
        scratch_shapes=[
            pltpu.VMEM((1, count), jnp.int32),
            pltpu.VMEM((1, count), jnp.int32),
            pltpu.VMEM((NODES, count), jnp.float32),
            pltpu.VMEM((1, 8), jnp.float32),
            pltpu.VMEM((16, 8, OWN), jnp.float32),
            pltpu.SemaphoreType.DMA((5,)),
        ],
        compiler_params=roomy,
        name="pack",
    )(core, block_owner.reshape(1, -1), block_cell.reshape(1, -1), density.T, cell_scale.reshape(1, -1), orbitals)
    other = lax.ppermute(send, "band", [(i, i ^ 1) for i in range(band_count)])
    own = pl.pallas_call(
        own_kernel,
        out_shape=jax.ShapeDtypeStruct((4 * SLAB, HALF), jnp.float32),
        in_specs=[vmem],
        out_specs=vmem,
        compiler_params=params,
        name="own_sums",
    )(own)
    delivered = pl.pallas_call(
        deliver_kernel,
        out_shape=jax.ShapeDtypeStruct((4 * SLAB, HALF), jnp.float32),
        in_specs=[vmem, vmem],
        out_specs=vmem,
        compiler_params=params,
        name="deliver",
    )(own, other)

    left = lax.ppermute(send_left, "dom", [(i, i + 1) for i in range(dom_count - 1)])
    right = lax.ppermute(send_right, "dom", [(i + 1, i) for i in range(dom_count - 1)])

    part = exchange(delivered.reshape(4, SLAB, HALF), "dom", X_GROUPS)
    windows = pl.pallas_call(
        window_kernel,
        out_shape=jax.ShapeDtypeStruct((16, PACKED, 128), jnp.float32),
        in_specs=[vmem],
        out_specs=vmem,
        scratch_shapes=[pltpu.VMEM((SLAB, HALF), jnp.float32)],
        compiler_params=params,
        name="windows",
    )(part)
    windows, left, right = lax.optimization_barrier((windows, left, right))
    part = exchange(windows, "dom", YZ_GROUPS)
    window = jnp.sum(part, 0)
    window, operator = lax.optimization_barrier((window, cell_operator))
    part = exchange(jnp.broadcast_to(window[None], (band_count, PACKED, 128)), "band")

    ksplit = pl.pallas_call(
        split_kernel,
        out_shape=jax.ShapeDtypeStruct((2 * WIDE, WIDE), jnp.bfloat16),
        in_specs=[vmem],
        out_specs=vmem,
        scratch_shapes=[pltpu.VMEM((WIDE, WIDE), jnp.float32)],
        compiler_params=params,
        name="split_operator",
    )(operator)
    filtered = pl.pallas_call(
        filter_kernel,
        out_shape=jax.ShapeDtypeStruct((8, 16, OWN), jnp.float32),
        in_specs=[smem] * 2 + [vmem] * 5,
        out_specs=vmem,
        scratch_shapes=[
            pltpu.VMEM((224, WIDE), jnp.float32),
            pltpu.VMEM((224, WIDE), jnp.float32),
            pltpu.VMEM((224, WIDE), jnp.float32),
            pltpu.VMEM((224, WIDE), jnp.bfloat16),
            pltpu.VMEM((224, WIDE), jnp.bfloat16),
            pltpu.VMEM((224, WIDE), jnp.float32),
            pltpu.VMEM((224, WIDE), jnp.float32),
            pltpu.VMEM((16, WIDE), jnp.float32),
        ],
        compiler_params=params,
        name="chebyshev",
    )(alive, cell_scale, orbitals, left, right, part, ksplit)

    flat = exchange(filtered, "band").reshape(128, OWN)
    both = ("dom", "band")
    total = OWN * dom_count * band_count
    gram = jnp.dot(flat, flat.T, precision=lax.Precision.HIGHEST)
    part = jnp.sum(exchange(gram.reshape(16, 8, 128), both, NEAR_GROUPS), 0)
    part = jnp.sum(exchange(jnp.broadcast_to(part[None], (32, 8, 128)), both, FAR_GROUPS), 0)
    gram = exchange(jnp.broadcast_to(part[None], (16, 8, 128)), both, NEAR_GROUPS).reshape(128, 128)
    basis = pl.pallas_call(
        functools.partial(solve_kernel, float(total)),
        out_shape=jax.ShapeDtypeStruct((OWN, 128), jnp.float32),
        in_specs=[vmem, vmem],
        out_specs=vmem,
        scratch_shapes=[pltpu.VMEM((128, 128), jnp.float32)],
        compiler_params=params,
        name="orthonormalize",
    )(gram, flat)
    return basis.T.reshape(128, 1, OWN)


def solution(mesh):
    return jax.shard_map(
        body,
        mesh=mesh,
        in_specs=(
            P("band", "dom", None),
            P(),
            P("dom"),
            P(("dom", "band"), None),
            P(("dom", "band"), None),
            P(("dom", "band")),
        ),
        out_specs=P(None, ("dom", "band"), None),
        check_vma=False,
    )
```

```python
import functools

import jax
import jax.numpy as jnp
from jax import lax
from jax.experimental import pallas as pl
from jax.experimental.pallas import tpu as pltpu
from jax.sharding import PartitionSpec as P

FACE = 81
OWN = 648
NODES = 729
WIDE = 768
HALF = 384
SLAB = 136
KEPT = 13
PACKED = 40
TILE5 = 640
SPLIT = OWN - TILE5

CENTER = -1.0
HALF_WIDTH = 2.5

X_GROUPS = [[x * 16 + r for x in range(4)] for r in range(16)]
YZ_GROUPS = [[x * 16 + r for r in range(16)] for x in range(4)]


def device(x, y, z_lo, z_hi, core):
    return ((x * 8 + y) * 2 + z_lo) * 8 + z_hi * 2 + core


NEAR_GROUPS = [[device(x, y, l, h, c) for x in range(4) for l in range(2) for c in range(2)]
               for y in range(8) for h in range(4)]
FAR_GROUPS = [[device(x, y, l, h, c) for y in range(8) for h in range(4)]
              for x in range(4) for l in range(2) for c in range(2)]


def exchange(value, axis, groups=None):
    return lax.all_to_all(value, axis, split_axis=0, concat_axis=0, tiled=True, axis_index_groups=groups)


def split2(value):
    high = value.astype(jnp.bfloat16)
    low = (value - high.astype(jnp.float32)).astype(jnp.bfloat16)
    return high, low


def dot(a, b):
    return jnp.dot(a, b, preferred_element_type=jnp.float32)


def dot_nt(a, b):
    return lax.dot_general(a, b, (((1,), (1,)), ((), ())), preferred_element_type=jnp.float32)


def pack_kernel(core_ref, owner_hbm, cell_hbm, density_hbm, own_ref, send_ref,
                owner_ref, cell_ref, density_ref, sems):
    copies = [
        pltpu.make_async_copy(density_hbm, density_ref, sems.at[0]),
        pltpu.make_async_copy(owner_hbm, owner_ref, sems.at[1]),
        pltpu.make_async_copy(cell_hbm, cell_ref, sems.at[2]),
    ]
    for copy in copies:
        copy.start()
    for copy in copies:
        copy.wait()

    count = density_ref.shape[1]
    target = (owner_ref[...] * 8 + cell_ref[...]).astype(jnp.float32)
    target = jnp.broadcast_to(target, (8, count))

    def lower(ref):
        ref[:HALF, :] = density_ref[:HALF, :]
        ref[HALF:, :] = target

    def upper(ref):
        ref[:344, :] = density_ref[HALF:728, :]
        ref[344:HALF, :] = jnp.zeros((HALF - 344, count), jnp.float32)
        ref[344:345, :] = density_ref[728:NODES, :]
        ref[HALF:, :] = target

    @pl.when(core_ref[0] == 0)
    def _():
        lower(own_ref)
        upper(send_ref)

    @pl.when(core_ref[0] != 0)
    def _():
        upper(own_ref)
        lower(send_ref)


def ghost_kernel(scale_ref, orbitals_ref, left_ref, right_ref):
    def ghost(ref, place, c):
        value = orbitals_ref[:, c, :]
        scale = jnp.broadcast_to(scale_ref[:, c:c + 1], (16, 128 - SPLIT))
        ref[:, WIDE * place:WIDE * place + TILE5] = value[:, :TILE5]
        ref[:, WIDE * place + TILE5:WIDE * place + WIDE] = jnp.concatenate([value[:, TILE5:], scale], 1)

    for place in range(3):
        ghost(left_ref, place, 5 + place)
    for place in range(2):
        ghost(right_ref, place, place)
    right_ref[:, 2 * WIDE:] = orbitals_ref[:, 2, :128]


def cell_sums(ref):
    rows = 4 * SLAB
    row = lax.broadcasted_iota(jnp.int32, (rows, ref.shape[1]), 0)
    slab = (row >= SLAB).astype(jnp.int32) + (row >= 2 * SLAB).astype(jnp.int32) + (row >= 3 * SLAB).astype(jnp.int32)
    cell = (row - 8 * slab - 3).astype(jnp.float32)
    onehot = jnp.where(ref[HALF:HALF + 1, :] == cell, 1.0, 0.0).astype(jnp.bfloat16)
    high, low = split2(ref[:HALF, :])
    return dot_nt(onehot, high) + dot_nt(onehot, low)


def own_kernel(own_ref, out_ref):
    out_ref[...] = cell_sums(own_ref)


def deliver_kernel(own_ref, other_ref, out_ref):
    out_ref[...] = own_ref[...] + cell_sums(other_ref)


def window_kernel(part_ref, out_ref, sum_ref):
    sum_ref[...] = (part_ref[0] + part_ref[1]) + (part_ref[2] + part_ref[3])
    for k in range(16):
        for t in range(3):
            out_ref[k, KEPT * t:KEPT * t + KEPT, :] = sum_ref[8 * k:8 * k + KEPT, 128 * t:128 * t + 128]
        out_ref[k, 3 * KEPT:, :] = jnp.zeros((PACKED - 3 * KEPT, 128), jnp.float32)


def cell_vectors(source, begin, end, cell_buf, chigh, clow):
    is_face = lax.broadcasted_iota(jnp.int32, (16, 128), 1) < FACE
    for i in range(begin, end):
        r = slice(16 * i, 16 * i + 16)
        n = slice(16 * i + 16, 16 * i + 32)
        for t in range(6):
            c = slice(128 * t, 128 * t + 128)
            value = source[r, c]
            if t == 5:
                face = jnp.where(is_face, source[n, :128], 0.0)
                value = value + pltpu.roll(face, SPLIT, 1)
            cell_buf[r, c] = value
            high, low = split2(value)
            chigh[r, c] = high
            clow[r, c] = low


def products(begin, end, product, chigh, clow, ksplit):
    r = slice(16 * begin, 16 * end)
    a, b = chigh[r, :], clow[r, :]
    khigh, klow = ksplit[:WIDE, :], ksplit[WIDE:, :]
    product[r, :] = dot(a, khigh) + dot(b, khigh) + dot(a, klow)


def first_vectors(own_ref, left_ref, right_ref, v0, cell_buf, chigh, clow):
    zero5 = jnp.zeros((16, WIDE - TILE5), jnp.float32)

    def place(i, value):
        v0[16 * i:16 * i + 16, TILE5:] = zero5
        v0[16 * i:16 * i + 16, :OWN] = value

    own_lane = lax.broadcasted_iota(jnp.int32, (16, 128), 1) < SPLIT

    def ghost(i, ref, begin):
        v0[16 * i:16 * i + 16, :TILE5] = ref[:, begin:begin + TILE5]
        v0[16 * i:16 * i + 16, TILE5:] = jnp.where(own_lane, ref[:, begin + TILE5:begin + WIDE], 0.0)

    for i in range(3):
        ghost(i, left_ref, WIDE * i)
    for i in range(2):
        ghost(11 + i, right_ref, WIDE * i)
    v0[16 * 13:, :128] = right_ref[:, 2 * WIDE:]
    for i in range(8):
        place(3 + i, own_ref[:, i, :])
    cell_vectors(v0, 0, 13, cell_buf, chigh, clow)


def split_kernel(operator_ref, ksplit, kwide):
    kwide[720:, :] = jnp.zeros((WIDE - 720, WIDE), jnp.float32)
    kwide[:, TILE5:] = jnp.zeros((WIDE, WIDE - TILE5), jnp.float32)
    kwide[:NODES, :NODES] = operator_ref[...]
    for i in range(0, WIDE, 128):
        high, low = split2(kwide[i:i + 128, :])
        ksplit[i:i + 128, :] = high
        ksplit[WIDE + i:WIDE + i + 128, :] = low


def filter_kernel(last_ref, scale_ref, own_ref, left_ref, right_ref, part_ref, ksplit, out_ref,
                  v0, v1, v2, chigh, clow, cell_buf, product, pot):
    for half in range(2):
        rho = (part_ref[half] + part_ref[half + 2]) + (part_ref[half + 4] + part_ref[half + 6])
        value = jnp.where(
            rho > 0.0, -0.7386 * jnp.exp(jnp.log(jnp.where(rho > 0.0, rho, 1.0)) * (1.0 / 3.0)), 0.0)
        for t in range(3):
            begin = half * HALF + 128 * t
            pot[:KEPT, begin:begin + 128] = value[KEPT * t:KEPT * t + KEPT, :]
    lane = lax.broadcasted_iota(jnp.int32, (16, 128), 1)
    is_face = lane < FACE
    is_own5 = lane < SPLIT

    def scale_of(i):
        if i < 3:
            line = left_ref[:, WIDE * i + OWN:WIDE * i + OWN + 1]
        elif i < 11:
            line = scale_ref[i - 3]
        else:
            line = right_ref[:, WIDE * (i - 11) + OWN:WIDE * (i - 11) + OWN + 1]
        return line

    alive = last_ref[0].astype(jnp.float32)

    def assemble(begin, end, product, cells, combine):
        tail = None
        for i in range(begin, end):
            r = slice(16 * i, 16 * i + 16)
            scale = scale_of(i)
            parts = []
            for t in range(6):
                c = slice(128 * t, 128 * t + 128)
                parts.append(scale * product[r, c] + pot[i:i + 1, c] * cells[r, c])
            if tail is not None:
                add = jnp.where(is_face, pltpu.roll(tail, 128 - SPLIT, 1), 0.0)
                if i == 11:
                    add = add * alive
                parts[0] = parts[0] + add
                for t in range(6):
                    value = parts[t]
                    if t == 5:
                        value = jnp.where(is_own5, value, 0.0)
                    combine(i, t, value)
            tail = parts[5]

    def apply(source, begin, end, combine):
        cell_vectors(source, begin, end, cell_buf, chigh, clow)
        products(begin, end, product, chigh, clow, ksplit)
        assemble(begin, end, product, cell_buf, combine)

    def at(ref, i, t):
        return ref[16 * i:16 * i + 16, 128 * t:128 * t + 128]

    def first(i, t, value):
        v1[16 * i:16 * i + 16, 128 * t:128 * t + 128] = (value - CENTER * at(v0, i, t)) * (1.0 / HALF_WIDTH)

    def second(i, t, value):
        v2[16 * i:16 * i + 16, 128 * t:128 * t + 128] = (value - CENTER * at(v1, i, t)) * (2.0 / HALF_WIDTH) - at(v0, i, t)

    def third(i, t, value):
        result = (value - CENTER * at(v2, i, t)) * (2.0 / HALF_WIDTH) - at(v1, i, t)
        if t < 5:
            out_ref[i - 3, :, 128 * t:128 * t + 128] = result
        else:
            out_ref[i - 3, :, TILE5:OWN] = result[:, :SPLIT]

    first_vectors(own_ref, left_ref, right_ref, v0, cell_buf, chigh, clow)
    products(0, 13, product, chigh, clow, ksplit)
    assemble(0, 13, product, cell_buf, first)
    apply(v1, 1, 12, second)
    apply(v2, 2, 11, third)


def solve_kernel(total, gram_ref, flat_ref, out_ref, inverse_ref):
    shape = (8, 128)
    col = lax.broadcasted_iota(jnp.int32, shape, 1)
    row = lax.broadcasted_iota(jnp.int32, shape, 0)
    a = [gram_ref[8 * i:8 * i + 8, :] * (1.0 / total) for i in range(16)]
    diagonal = [jnp.where(col == row + 8 * i, a[i], 0.0) for i in range(16)]
    across = jnp.broadcast_to(lax.rsqrt(jnp.sum(sum(diagonal), 0, keepdims=True)), shape)
    a = [a[i] * lax.rsqrt(jnp.sum(diagonal[i], 1, keepdims=True)) * across for i in range(16)]
    w = [jnp.where(col == row + 8 * i, 1.0, 0.0) for i in range(16)]

    def columns(block, k):
        return [jnp.broadcast_to(block[:, 8 * k + j:8 * k + j + 1], shape) for j in range(8)]

    def line(block, i):
        return jnp.broadcast_to(block[i:i + 1, :], shape)

    for k in range(16):
        own = columns(a[k], k)
        s = [[line(own[j], i) for j in range(i + 1)] for i in range(8)]
        low = [[None] * 8 for _ in range(8)]
        inv = [None] * 8
        for j in range(0, 8, 2):
            inv[j] = 1.0 / s[j][j]
            inv[j + 1] = s[j][j] * (1.0 / (s[j][j] * s[j + 1][j + 1] - s[j + 1][j] * s[j + 1][j]))
            for i in range(j + 1, 8):
                low[i][j] = s[i][j] * inv[j]
            for i in range(j + 2, 8):
                s[i][j + 1] = s[i][j + 1] - low[i][j] * s[j + 1][j]
                low[i][j + 1] = s[i][j + 1] * inv[j + 1]
            for i in range(j + 2, 8):
                for m in range(j + 2, i + 1):
                    s[i][m] = s[i][m] - low[i][j] * s[m][j] - low[i][j + 1] * s[m][j + 1]
        n = [[None] * 8 for _ in range(8)]
        for i in range(8):
            for j in range(i):
                value = low[i][j]
                for m in range(j + 1, i):
                    value = value + low[i][m] * n[m][j]
                n[i][j] = -value

        def forward(block):
            lines = [line(block, i) for i in range(8)]
            result = []
            for i in range(8):
                value = lines[i]
                for j in range(i):
                    value = value + n[i][j] * lines[j]
                result.append(value)
            return result

        def backward(lines):
            scaled = [inv[i] * lines[i] for i in range(8)]
            result = []
            for j in range(8):
                value = scaled[j]
                for i in range(j + 1, 8):
                    value = value + n[i][j] * scaled[i]
                result.append(value)
            return result

        lines_w = forward(w[k])
        final = jnp.zeros(shape, jnp.float32)
        for i in range(8):
            final = jnp.where(row == i, lines_w[i] * jnp.sqrt(inv[i]), final)
        inverse_ref[8 * k:8 * k + 8, :] = final * across
        if k < 15:
            za = backward(forward(a[k]))
            zw = backward(lines_w)
            for i in range(k + 1, 16):
                c = columns(a[i], k)
                for j in range(8):
                    a[i] = a[i] - c[j] * za[j]
                    w[i] = w[i] - c[j] * zw[j]
    inverse_high, inverse_low = split2(inverse_ref[...])
    for begin in range(0, OWN, 128):
        c = slice(begin, min(begin + 128, OWN))
        flat_high, flat_low = split2(jnp.transpose(flat_ref[:, c]))
        out_ref[c, :] = (dot_nt(flat_high, inverse_high) + dot_nt(flat_low, inverse_high)
                         + dot_nt(flat_high, inverse_low))


def body(orbitals, cell_operator, cell_scale, density, block_owner, block_cell):
    dom_count = lax.axis_size("dom")
    band_count = lax.axis_size("band")
    dom = lax.axis_index("dom")
    core = jnp.reshape(lax.axis_index("band") % 2, (1,)).astype(jnp.int32)
    alive = jnp.reshape((dom < dom_count - 1).astype(jnp.int32), (1,))
    smem = pl.BlockSpec(memory_space=pltpu.SMEM)
    vmem = pl.BlockSpec(memory_space=pltpu.VMEM)
    hbm = pl.BlockSpec(memory_space=pltpu.HBM)
    params = pltpu.CompilerParams(vmem_limit_bytes=16 << 20)
    roomy = pltpu.CompilerParams(vmem_limit_bytes=62 << 20)

    count = density.shape[0]
    pack_shape = jax.ShapeDtypeStruct((HALF + 8, count), jnp.float32)
    left_shape = jax.ShapeDtypeStruct((16, 3 * WIDE), jnp.float32)
    right_shape = jax.ShapeDtypeStruct((16, 2 * WIDE + 128), jnp.float32)
    own, send = pl.pallas_call(
        pack_kernel,
        out_shape=(pack_shape, pack_shape),
        in_specs=[smem] + [hbm] * 3,
        out_specs=(vmem,) * 2,
        scratch_shapes=[
            pltpu.VMEM((1, count), jnp.int32),
            pltpu.VMEM((1, count), jnp.int32),
            pltpu.VMEM((NODES, count), jnp.float32),
            pltpu.SemaphoreType.DMA((3,)),
        ],
        compiler_params=roomy,
        name="pack",
    )(core, block_owner.reshape(1, -1), block_cell.reshape(1, -1), density.T)
    other = lax.ppermute(send, "band", [(i, i ^ 1) for i in range(band_count)])
    own = pl.pallas_call(
        own_kernel,
        out_shape=jax.ShapeDtypeStruct((4 * SLAB, HALF), jnp.float32),
        in_specs=[vmem],
        out_specs=vmem,
        compiler_params=params,
        name="own_sums",
    )(own)
    delivered = pl.pallas_call(
        deliver_kernel,
        out_shape=jax.ShapeDtypeStruct((4 * SLAB, HALF), jnp.float32),
        in_specs=[vmem, vmem],
        out_specs=vmem,
        compiler_params=params,
        name="deliver",
    )(own, other)

    send_left, send_right = pl.pallas_call(
        ghost_kernel,
        out_shape=(left_shape, right_shape),
        in_specs=[vmem, vmem],
        out_specs=(vmem, vmem),
        compiler_params=params,
        name="ghosts",
    )(cell_scale.reshape(1, -1), orbitals)
    left = lax.ppermute(send_left, "dom", [(i, i + 1) for i in range(dom_count - 1)])
    right = lax.ppermute(send_right, "dom", [(i + 1, i) for i in range(dom_count - 1)])

    part = exchange(delivered.reshape(4, SLAB, HALF), "dom", X_GROUPS)
    windows = pl.pallas_call(
        window_kernel,
        out_shape=jax.ShapeDtypeStruct((16, PACKED, 128), jnp.float32),
        in_specs=[vmem],
        out_specs=vmem,
        scratch_shapes=[pltpu.VMEM((SLAB, HALF), jnp.float32)],
        compiler_params=params,
        name="windows",
    )(part)
    windows, left, right = lax.optimization_barrier((windows, left, right))
    part = exchange(windows, "dom", YZ_GROUPS)
    window = jnp.sum(part, 0)
    window, operator = lax.optimization_barrier((window, cell_operator))
    part = exchange(jnp.broadcast_to(window[None], (band_count, PACKED, 128)), "band")

    ksplit = pl.pallas_call(
        split_kernel,
        out_shape=jax.ShapeDtypeStruct((2 * WIDE, WIDE), jnp.bfloat16),
        in_specs=[vmem],
        out_specs=vmem,
        scratch_shapes=[pltpu.VMEM((WIDE, WIDE), jnp.float32)],
        compiler_params=params,
        name="split_operator",
    )(operator)
    filtered = pl.pallas_call(
        filter_kernel,
        out_shape=jax.ShapeDtypeStruct((8, 16, OWN), jnp.float32),
        in_specs=[smem] * 2 + [vmem] * 5,
        out_specs=vmem,
        scratch_shapes=[
            pltpu.VMEM((224, WIDE), jnp.float32),
            pltpu.VMEM((224, WIDE), jnp.float32),
            pltpu.VMEM((224, WIDE), jnp.float32),
            pltpu.VMEM((224, WIDE), jnp.bfloat16),
            pltpu.VMEM((224, WIDE), jnp.bfloat16),
            pltpu.VMEM((224, WIDE), jnp.float32),
            pltpu.VMEM((224, WIDE), jnp.float32),
            pltpu.VMEM((16, WIDE), jnp.float32),
        ],
        compiler_params=params,
        name="chebyshev",
    )(alive, cell_scale, orbitals, left, right, part, ksplit)

    flat = exchange(filtered, "band").reshape(128, OWN)
    both = ("dom", "band")
    total = OWN * dom_count * band_count
    gram = jnp.dot(flat, flat.T, precision=lax.Precision.HIGHEST)
    part = jnp.sum(exchange(gram.reshape(16, 8, 128), both, NEAR_GROUPS), 0)
    part = jnp.sum(exchange(jnp.broadcast_to(part[None], (32, 8, 128)), both, FAR_GROUPS), 0)
    gram = exchange(jnp.broadcast_to(part[None], (16, 8, 128)), both, NEAR_GROUPS).reshape(128, 128)
    basis = pl.pallas_call(
        functools.partial(solve_kernel, float(total)),
        out_shape=jax.ShapeDtypeStruct((OWN, 128), jnp.float32),
        in_specs=[vmem, vmem],
        out_specs=vmem,
        scratch_shapes=[pltpu.VMEM((128, 128), jnp.float32)],
        compiler_params=params,
        name="orthonormalize",
    )(gram, flat)
    return basis.T.reshape(128, 1, OWN)


def solution(mesh):
    return jax.shard_map(
        body,
        mesh=mesh,
        in_specs=(
            P("band", "dom", None),
            P(),
            P("dom"),
            P(("dom", "band"), None),
            P(("dom", "band"), None),
            P(("dom", "band")),
        ),
        out_specs=P(None, ("dom", "band"), None),
        check_vma=False,
    )
```

```python
import functools

import jax
import jax.numpy as jnp
from jax import lax
from jax.experimental import pallas as pl
from jax.experimental.pallas import tpu as pltpu
from jax.sharding import PartitionSpec as P

FACE = 81
OWN = 648
NODES = 729
WIDE = 768
HALF = 384
SLAB = 136
KEPT = 13
PACKED = 40
TILE5 = 640
SPLIT = OWN - TILE5

CENTER = -1.0
HALF_WIDTH = 2.5

X_GROUPS = [[x * 16 + r for x in range(4)] for r in range(16)]
YZ_GROUPS = [[x * 16 + r for r in range(16)] for x in range(4)]


def device(x, y, z_lo, z_hi, core):
    return ((x * 8 + y) * 2 + z_lo) * 8 + z_hi * 2 + core


NEAR_GROUPS = [[device(x, y, l, h, c) for x in range(4) for l in range(2) for c in range(2)]
               for y in range(8) for h in range(4)]
FAR_GROUPS = [[device(x, y, l, h, c) for y in range(8) for h in range(4)]
              for x in range(4) for l in range(2) for c in range(2)]


def exchange(value, axis, groups=None):
    return lax.all_to_all(value, axis, split_axis=0, concat_axis=0, tiled=True, axis_index_groups=groups)


def split2(value):
    high = value.astype(jnp.bfloat16)
    low = (value - high.astype(jnp.float32)).astype(jnp.bfloat16)
    return high, low


def dot(a, b):
    return jnp.dot(a, b, preferred_element_type=jnp.float32)


def dot_nt(a, b):
    return lax.dot_general(a, b, (((1,), (1,)), ((), ())), preferred_element_type=jnp.float32)


def pack_kernel(core_ref, owner_hbm, cell_hbm, density_hbm, own_ref, send_ref,
                owner_ref, cell_ref, density_ref, sems):
    copies = [
        pltpu.make_async_copy(density_hbm, density_ref, sems.at[0]),
        pltpu.make_async_copy(owner_hbm, owner_ref, sems.at[1]),
        pltpu.make_async_copy(cell_hbm, cell_ref, sems.at[2]),
    ]
    for copy in copies:
        copy.start()
    for copy in copies:
        copy.wait()

    count = density_ref.shape[1]
    target = (owner_ref[...] * 8 + cell_ref[...]).astype(jnp.float32)
    target = jnp.broadcast_to(target, (8, count))

    def lower(ref):
        ref[:HALF, :] = density_ref[:HALF, :]
        ref[HALF:, :] = target

    def upper(ref):
        ref[:344, :] = density_ref[HALF:728, :]
        ref[344:HALF, :] = jnp.zeros((HALF - 344, count), jnp.float32)
        ref[344:345, :] = density_ref[728:NODES, :]
        ref[HALF:, :] = target

    @pl.when(core_ref[0] == 0)
    def _():
        lower(own_ref)
        upper(send_ref)

    @pl.when(core_ref[0] != 0)
    def _():
        upper(own_ref)
        lower(send_ref)


def ghost_kernel(scale_ref, orbitals_ref, left_ref, right_ref):
    def ghost(ref, place, c):
        value = orbitals_ref[:, c, :]
        scale = jnp.broadcast_to(scale_ref[:, c:c + 1], (16, 128 - SPLIT))
        ref[:, WIDE * place:WIDE * place + TILE5] = value[:, :TILE5]
        ref[:, WIDE * place + TILE5:WIDE * place + WIDE] = jnp.concatenate([value[:, TILE5:], scale], 1)

    for place in range(3):
        ghost(left_ref, place, 5 + place)
    for place in range(2):
        ghost(right_ref, place, place)
    right_ref[:, 2 * WIDE:] = orbitals_ref[:, 2, :128]


def cell_sums(ref):
    rows = 4 * SLAB
    row = lax.broadcasted_iota(jnp.int32, (rows, ref.shape[1]), 0)
    slab = (row >= SLAB).astype(jnp.int32) + (row >= 2 * SLAB).astype(jnp.int32) + (row >= 3 * SLAB).astype(jnp.int32)
    cell = (row - 8 * slab - 3).astype(jnp.float32)
    onehot = jnp.where(ref[HALF:HALF + 1, :] == cell, 1.0, 0.0).astype(jnp.bfloat16)
    high, low = split2(ref[:HALF, :])
    return dot_nt(onehot, high) + dot_nt(onehot, low)


def own_kernel(own_ref, out_ref):
    out_ref[...] = cell_sums(own_ref)


def deliver_kernel(own_ref, other_ref, out_ref):
    out_ref[...] = own_ref[...] + cell_sums(other_ref)


def window_kernel(part_ref, out_ref, sum_ref):
    sum_ref[...] = (part_ref[0] + part_ref[1]) + (part_ref[2] + part_ref[3])
    for k in range(16):
        for t in range(3):
            out_ref[k, KEPT * t:KEPT * t + KEPT, :] = sum_ref[8 * k:8 * k + KEPT, 128 * t:128 * t + 128]
        out_ref[k, 3 * KEPT:, :] = jnp.zeros((PACKED - 3 * KEPT, 128), jnp.float32)


def cell_vectors(source, begin, end, cell_buf, chigh, clow):
    is_face = lax.broadcasted_iota(jnp.int32, (16, 128), 1) < FACE
    for i in range(begin, end):
        r = slice(16 * i, 16 * i + 16)
        n = slice(16 * i + 16, 16 * i + 32)
        for t in range(6):
            c = slice(128 * t, 128 * t + 128)
            value = source[r, c]
            if t == 5:
                face = jnp.where(is_face, source[n, :128], 0.0)
                value = value + pltpu.roll(face, SPLIT, 1)
            cell_buf[r, c] = value
            high, low = split2(value)
            chigh[r, c] = high
            clow[r, c] = low


def products(begin, end, product, chigh, clow, ksplit):
    r = slice(16 * begin, 16 * end)
    a, b = chigh[r, :], clow[r, :]
    khigh, klow = ksplit[:WIDE, :], ksplit[WIDE:, :]
    product[r, :] = dot(a, khigh) + dot(b, khigh) + dot(a, klow)


def first_vectors(own_ref, left_ref, right_ref, v0, cell_buf, chigh, clow):
    zero5 = jnp.zeros((16, WIDE - TILE5), jnp.float32)

    def place(i, value):
        v0[16 * i:16 * i + 16, TILE5:] = zero5
        v0[16 * i:16 * i + 16, :OWN] = value

    own_lane = lax.broadcasted_iota(jnp.int32, (16, 128), 1) < SPLIT

    def ghost(i, ref, begin):
        v0[16 * i:16 * i + 16, :TILE5] = ref[:, begin:begin + TILE5]
        v0[16 * i:16 * i + 16, TILE5:] = jnp.where(own_lane, ref[:, begin + TILE5:begin + WIDE], 0.0)

    for i in range(3):
        ghost(i, left_ref, WIDE * i)
    for i in range(2):
        ghost(11 + i, right_ref, WIDE * i)
    v0[16 * 13:, :128] = right_ref[:, 2 * WIDE:]
    for i in range(8):
        place(3 + i, own_ref[:, i, :])
    cell_vectors(v0, 0, 13, cell_buf, chigh, clow)


def split_kernel(operator_ref, ksplit, kwide):
    kwide[720:, :] = jnp.zeros((WIDE - 720, WIDE), jnp.float32)
    kwide[:, TILE5:] = jnp.zeros((WIDE, WIDE - TILE5), jnp.float32)
    kwide[:NODES, :NODES] = operator_ref[...]
    for i in range(0, WIDE, 128):
        high, low = split2(kwide[i:i + 128, :])
        ksplit[i:i + 128, :] = high
        ksplit[WIDE + i:WIDE + i + 128, :] = low


def filter_kernel(last_ref, scale_ref, own_ref, left_ref, right_ref, part_ref, ksplit, out_ref,
                  v0, v1, v2, chigh, clow, cell_buf, product, pot):
    for half in range(2):
        rho = (part_ref[half] + part_ref[half + 2]) + (part_ref[half + 4] + part_ref[half + 6])
        value = jnp.where(
            rho > 0.0, -0.7386 * jnp.exp(jnp.log(jnp.where(rho > 0.0, rho, 1.0)) * (1.0 / 3.0)), 0.0)
        for t in range(3):
            begin = half * HALF + 128 * t
            pot[:KEPT, begin:begin + 128] = value[KEPT * t:KEPT * t + KEPT, :]
    lane = lax.broadcasted_iota(jnp.int32, (16, 128), 1)
    is_face = lane < FACE
    is_own5 = lane < SPLIT

    def scale_of(i):
        if i < 3:
            line = left_ref[:, WIDE * i + OWN:WIDE * i + OWN + 1]
        elif i < 11:
            line = scale_ref[i - 3]
        else:
            line = right_ref[:, WIDE * (i - 11) + OWN:WIDE * (i - 11) + OWN + 1]
        return line

    alive = last_ref[0].astype(jnp.float32)

    def assemble(begin, end, product, cells, combine):
        tail = None
        for i in range(begin, end):
            r = slice(16 * i, 16 * i + 16)
            scale = scale_of(i)
            parts = []
            for t in range(6):
                c = slice(128 * t, 128 * t + 128)
                parts.append(scale * product[r, c] + pot[i:i + 1, c] * cells[r, c])
            if tail is not None:
                add = jnp.where(is_face, pltpu.roll(tail, 128 - SPLIT, 1), 0.0)
                if i == 11:
                    add = add * alive
                parts[0] = parts[0] + add
                for t in range(6):
                    value = parts[t]
                    if t == 5:
                        value = jnp.where(is_own5, value, 0.0)
                    combine(i, t, value)
            tail = parts[5]

    def apply(source, begin, end, combine):
        cell_vectors(source, begin, end, cell_buf, chigh, clow)
        products(begin, end, product, chigh, clow, ksplit)
        assemble(begin, end, product, cell_buf, combine)

    def at(ref, i, t):
        return ref[16 * i:16 * i + 16, 128 * t:128 * t + 128]

    def first(i, t, value):
        v1[16 * i:16 * i + 16, 128 * t:128 * t + 128] = (value - CENTER * at(v0, i, t)) * (1.0 / HALF_WIDTH)

    def second(i, t, value):
        v2[16 * i:16 * i + 16, 128 * t:128 * t + 128] = (value - CENTER * at(v1, i, t)) * (2.0 / HALF_WIDTH) - at(v0, i, t)

    def third(i, t, value):
        result = (value - CENTER * at(v2, i, t)) * (2.0 / HALF_WIDTH) - at(v1, i, t)
        if t < 5:
            out_ref[i - 3, :, 128 * t:128 * t + 128] = result
        else:
            out_ref[i - 3, :, TILE5:OWN] = result[:, :SPLIT]

    first_vectors(own_ref, left_ref, right_ref, v0, cell_buf, chigh, clow)
    products(0, 13, product, chigh, clow, ksplit)
    assemble(0, 13, product, cell_buf, first)
    apply(v1, 1, 12, second)
    apply(v2, 2, 11, third)


def solve_kernel(total, gram_ref, flat_ref, out_ref, inverse_ref):
    shape = (8, 128)
    col = lax.broadcasted_iota(jnp.int32, shape, 1)
    row = lax.broadcasted_iota(jnp.int32, shape, 0)
    a = [gram_ref[8 * i:8 * i + 8, :] * (1.0 / total) for i in range(16)]
    w = [jnp.where(col == row + 8 * i, 1.0, 0.0) for i in range(16)]

    def columns(block, k):
        return [jnp.broadcast_to(block[:, 8 * k + j:8 * k + j + 1], shape) for j in range(8)]

    def line(block, i):
        return jnp.broadcast_to(block[i:i + 1, :], shape)

    for k in range(16):
        own = columns(a[k], k)
        s = [[line(own[j], i) for j in range(i + 1)] for i in range(8)]
        low = [[None] * 8 for _ in range(8)]
        inv = [None] * 8
        for j in range(8):
            inv[j] = 1.0 / s[j][j]
            for i in range(j + 1, 8):
                low[i][j] = s[i][j] * inv[j]
            for i in range(j + 1, 8):
                for m in range(j + 1, i + 1):
                    s[i][m] = s[i][m] - low[i][j] * s[m][j]
        n = [[None] * 8 for _ in range(8)]
        for i in range(8):
            for j in range(i):
                value = low[i][j]
                for m in range(j + 1, i):
                    value = value + low[i][m] * n[m][j]
                n[i][j] = -value

        def forward(block):
            lines = [line(block, i) for i in range(8)]
            result = []
            for i in range(8):
                value = lines[i]
                for j in range(i):
                    value = value + n[i][j] * lines[j]
                result.append(value)
            return result

        def backward(lines):
            scaled = [inv[i] * lines[i] for i in range(8)]
            result = []
            for j in range(8):
                value = scaled[j]
                for i in range(j + 1, 8):
                    value = value + n[i][j] * scaled[i]
                result.append(value)
            return result

        lines_w = forward(w[k])
        final = jnp.zeros(shape, jnp.float32)
        for i in range(8):
            final = jnp.where(row == i, lines_w[i] * jnp.sqrt(inv[i]), final)
        inverse_ref[8 * k:8 * k + 8, :] = final
        if k < 15:
            za = backward(forward(a[k]))
            zw = backward(lines_w)
            for i in range(k + 1, 16):
                c = columns(a[i], k)
                for j in range(8):
                    a[i] = a[i] - c[j] * za[j]
                    w[i] = w[i] - c[j] * zw[j]
    inverse_high, inverse_low = split2(inverse_ref[...])
    for begin in range(0, OWN, 128):
        c = slice(begin, min(begin + 128, OWN))
        flat_high, flat_low = split2(jnp.transpose(flat_ref[:, c]))
        out_ref[c, :] = (dot_nt(flat_high, inverse_high) + dot_nt(flat_low, inverse_high)
                         + dot_nt(flat_high, inverse_low))


def body(orbitals, cell_operator, cell_scale, density, block_owner, block_cell):
    dom_count = lax.axis_size("dom")
    band_count = lax.axis_size("band")
    dom = lax.axis_index("dom")
    core = jnp.reshape(lax.axis_index("band") % 2, (1,)).astype(jnp.int32)
    alive = jnp.reshape((dom < dom_count - 1).astype(jnp.int32), (1,))
    smem = pl.BlockSpec(memory_space=pltpu.SMEM)
    vmem = pl.BlockSpec(memory_space=pltpu.VMEM)
    hbm = pl.BlockSpec(memory_space=pltpu.HBM)
    params = pltpu.CompilerParams(vmem_limit_bytes=16 << 20)
    roomy = pltpu.CompilerParams(vmem_limit_bytes=62 << 20)

    count = density.shape[0]
    pack_shape = jax.ShapeDtypeStruct((HALF + 8, count), jnp.float32)
    left_shape = jax.ShapeDtypeStruct((16, 3 * WIDE), jnp.float32)
    right_shape = jax.ShapeDtypeStruct((16, 2 * WIDE + 128), jnp.float32)
    own, send = pl.pallas_call(
        pack_kernel,
        out_shape=(pack_shape, pack_shape),
        in_specs=[smem] + [hbm] * 3,
        out_specs=(vmem,) * 2,
        scratch_shapes=[
            pltpu.VMEM((1, count), jnp.int32),
            pltpu.VMEM((1, count), jnp.int32),
            pltpu.VMEM((NODES, count), jnp.float32),
            pltpu.SemaphoreType.DMA((3,)),
        ],
        compiler_params=roomy,
        name="pack",
    )(core, block_owner.reshape(1, -1), block_cell.reshape(1, -1), density.T)
    other = lax.ppermute(send, "band", [(i, i ^ 1) for i in range(band_count)])
    own = pl.pallas_call(
        own_kernel,
        out_shape=jax.ShapeDtypeStruct((4 * SLAB, HALF), jnp.float32),
        in_specs=[vmem],
        out_specs=vmem,
        compiler_params=params,
        name="own_sums",
    )(own)
    delivered = pl.pallas_call(
        deliver_kernel,
        out_shape=jax.ShapeDtypeStruct((4 * SLAB, HALF), jnp.float32),
        in_specs=[vmem, vmem],
        out_specs=vmem,
        compiler_params=params,
        name="deliver",
    )(own, other)

    send_left, send_right = pl.pallas_call(
        ghost_kernel,
        out_shape=(left_shape, right_shape),
        in_specs=[vmem, vmem],
        out_specs=(vmem, vmem),
        compiler_params=params,
        name="ghosts",
    )(cell_scale.reshape(1, -1), orbitals)
    left = lax.ppermute(send_left, "dom", [(i, i + 1) for i in range(dom_count - 1)])
    right = lax.ppermute(send_right, "dom", [(i + 1, i) for i in range(dom_count - 1)])

    part = exchange(delivered.reshape(4, SLAB, HALF), "dom", X_GROUPS)
    windows = pl.pallas_call(
        window_kernel,
        out_shape=jax.ShapeDtypeStruct((16, PACKED, 128), jnp.float32),
        in_specs=[vmem],
        out_specs=vmem,
        scratch_shapes=[pltpu.VMEM((SLAB, HALF), jnp.float32)],
        compiler_params=params,
        name="windows",
    )(part)
    windows, left, right = lax.optimization_barrier((windows, left, right))
    part = exchange(windows, "dom", YZ_GROUPS)
    window = jnp.sum(part, 0)
    window, operator = lax.optimization_barrier((window, cell_operator))
    part = exchange(jnp.broadcast_to(window[None], (band_count, PACKED, 128)), "band")

    ksplit = pl.pallas_call(
        split_kernel,
        out_shape=jax.ShapeDtypeStruct((2 * WIDE, WIDE), jnp.bfloat16),
        in_specs=[vmem],
        out_specs=vmem,
        scratch_shapes=[pltpu.VMEM((WIDE, WIDE), jnp.float32)],
        compiler_params=params,
        name="split_operator",
    )(operator)
    filtered = pl.pallas_call(
        filter_kernel,
        out_shape=jax.ShapeDtypeStruct((8, 16, OWN), jnp.float32),
        in_specs=[smem] * 2 + [vmem] * 5,
        out_specs=vmem,
        scratch_shapes=[
            pltpu.VMEM((224, WIDE), jnp.float32),
            pltpu.VMEM((224, WIDE), jnp.float32),
            pltpu.VMEM((224, WIDE), jnp.float32),
            pltpu.VMEM((224, WIDE), jnp.bfloat16),
            pltpu.VMEM((224, WIDE), jnp.bfloat16),
            pltpu.VMEM((224, WIDE), jnp.float32),
            pltpu.VMEM((224, WIDE), jnp.float32),
            pltpu.VMEM((16, WIDE), jnp.float32),
        ],
        compiler_params=params,
        name="chebyshev",
    )(alive, cell_scale, orbitals, left, right, part, ksplit)

    flat = exchange(filtered, "band").reshape(128, OWN)
    both = ("dom", "band")
    total = OWN * dom_count * band_count
    gram = jnp.dot(flat, flat.T, precision=lax.Precision.HIGH)
    part = jnp.sum(exchange(gram.reshape(16, 8, 128), both, NEAR_GROUPS), 0)
    part = jnp.sum(exchange(jnp.broadcast_to(part[None], (32, 8, 128)), both, FAR_GROUPS), 0)
    gram = exchange(jnp.broadcast_to(part[None], (16, 8, 128)), both, NEAR_GROUPS).reshape(128, 128)
    basis = pl.pallas_call(
        functools.partial(solve_kernel, float(total)),
        out_shape=jax.ShapeDtypeStruct((OWN, 128), jnp.float32),
        in_specs=[vmem, vmem],
        out_specs=vmem,
        scratch_shapes=[pltpu.VMEM((128, 128), jnp.float32)],
        compiler_params=params,
        name="orthonormalize",
    )(gram, flat)
    return basis.T.reshape(128, 1, OWN)


def solution(mesh):
    return jax.shard_map(
        body,
        mesh=mesh,
        in_specs=(
            P("band", "dom", None),
            P(),
            P("dom"),
            P(("dom", "band"), None),
            P(("dom", "band"), None),
            P(("dom", "band")),
        ),
        out_specs=P(None, ("dom", "band"), None),
        check_vma=False,
    )
```

```python
import functools

import jax
import jax.numpy as jnp
from jax import lax
from jax.experimental import pallas as pl
from jax.experimental.pallas import tpu as pltpu
from jax.sharding import PartitionSpec as P

FACE = 81
OWN = 648
NODES = 729
WIDE = 768
HALF = 384
SLAB = 136
KEPT = 13
PACKED = 40
TILE5 = 640
SPLIT = OWN - TILE5

CENTER = -1.0
HALF_WIDTH = 2.5

X_GROUPS = [[x * 16 + r for x in range(4)] for r in range(16)]
YZ_GROUPS = [[x * 16 + r for r in range(16)] for x in range(4)]


def device(x, y, z_lo, z_hi, core):
    return ((x * 8 + y) * 2 + z_lo) * 8 + z_hi * 2 + core


NEAR_GROUPS = [[device(x, y, l, h, c) for x in range(4) for l in range(2) for c in range(2)]
               for y in range(8) for h in range(4)]
FAR_GROUPS = [[device(x, y, l, h, c) for y in range(8) for h in range(4)]
              for x in range(4) for l in range(2) for c in range(2)]


def exchange(value, axis, groups=None):
    return lax.all_to_all(value, axis, split_axis=0, concat_axis=0, tiled=True, axis_index_groups=groups)


def split2(value):
    high = value.astype(jnp.bfloat16)
    low = (value - high.astype(jnp.float32)).astype(jnp.bfloat16)
    return high, low


def dot(a, b):
    return jnp.dot(a, b, preferred_element_type=jnp.float32)


def dot_nt(a, b):
    return lax.dot_general(a, b, (((1,), (1,)), ((), ())), preferred_element_type=jnp.float32)


def pack_kernel(core_ref, owner_hbm, cell_hbm, density_hbm, own_ref, send_ref,
                owner_ref, cell_ref, density_ref, sems):
    copies = [
        pltpu.make_async_copy(density_hbm, density_ref, sems.at[0]),
        pltpu.make_async_copy(owner_hbm, owner_ref, sems.at[1]),
        pltpu.make_async_copy(cell_hbm, cell_ref, sems.at[2]),
    ]
    for copy in copies:
        copy.start()
    for copy in copies:
        copy.wait()

    count = density_ref.shape[1]
    target = (owner_ref[...] * 8 + cell_ref[...]).astype(jnp.float32)
    target = jnp.broadcast_to(target, (8, count))

    def lower(ref):
        ref[:HALF, :] = density_ref[:HALF, :]
        ref[HALF:, :] = target

    def upper(ref):
        ref[:344, :] = density_ref[HALF:728, :]
        ref[344:HALF, :] = jnp.zeros((HALF - 344, count), jnp.float32)
        ref[344:345, :] = density_ref[728:NODES, :]
        ref[HALF:, :] = target

    @pl.when(core_ref[0] == 0)
    def _():
        lower(own_ref)
        upper(send_ref)

    @pl.when(core_ref[0] != 0)
    def _():
        upper(own_ref)
        lower(send_ref)


def ghost_kernel(scale_ref, orbitals_ref, left_ref, right_ref):
    def ghost(ref, place, c):
        value = orbitals_ref[:, c, :]
        scale = jnp.broadcast_to(scale_ref[:, c:c + 1], (16, 128 - SPLIT))
        ref[:, WIDE * place:WIDE * place + TILE5] = value[:, :TILE5]
        ref[:, WIDE * place + TILE5:WIDE * place + WIDE] = jnp.concatenate([value[:, TILE5:], scale], 1)

    for place in range(3):
        ghost(left_ref, place, 5 + place)
    for place in range(2):
        ghost(right_ref, place, place)
    right_ref[:, 2 * WIDE:] = orbitals_ref[:, 2, :128]


def cell_sums(ref):
    rows = 4 * SLAB
    row = lax.broadcasted_iota(jnp.int32, (rows, ref.shape[1]), 0)
    slab = (row >= SLAB).astype(jnp.int32) + (row >= 2 * SLAB).astype(jnp.int32) + (row >= 3 * SLAB).astype(jnp.int32)
    cell = (row - 8 * slab - 3).astype(jnp.float32)
    onehot = jnp.where(ref[HALF:HALF + 1, :] == cell, 1.0, 0.0).astype(jnp.bfloat16)
    high, low = split2(ref[:HALF, :])
    return dot_nt(onehot, high) + dot_nt(onehot, low)


def own_kernel(own_ref, out_ref):
    out_ref[...] = cell_sums(own_ref)


def deliver_kernel(own_ref, other_ref, out_ref):
    out_ref[...] = own_ref[...] + cell_sums(other_ref)


def window_kernel(part_ref, out_ref, sum_ref):
    sum_ref[...] = (part_ref[0] + part_ref[1]) + (part_ref[2] + part_ref[3])
    for k in range(16):
        for t in range(3):
            out_ref[k, KEPT * t:KEPT * t + KEPT, :] = sum_ref[8 * k:8 * k + KEPT, 128 * t:128 * t + 128]
        out_ref[k, 3 * KEPT:, :] = jnp.zeros((PACKED - 3 * KEPT, 128), jnp.float32)


def cell_vectors(source, begin, end, cell_buf, chigh, clow):
    is_face = lax.broadcasted_iota(jnp.int32, (16, 128), 1) < FACE
    for i in range(begin, end):
        r = slice(16 * i, 16 * i + 16)
        n = slice(16 * i + 16, 16 * i + 32)
        for t in range(6):
            c = slice(128 * t, 128 * t + 128)
            value = source[r, c]
            if t == 5:
                face = jnp.where(is_face, source[n, :128], 0.0)
                value = value + pltpu.roll(face, SPLIT, 1)
            cell_buf[r, c] = value
            high, low = split2(value)
            chigh[r, c] = high
            clow[r, c] = low


def products(begin, end, product, chigh, clow, ksplit):
    r = slice(16 * begin, 16 * end)
    a, b = chigh[r, :], clow[r, :]
    khigh, klow = ksplit[:WIDE, :], ksplit[WIDE:, :]
    product[r, :] = dot(a, khigh) + dot(b, khigh) + dot(a, klow)


def first_vectors(own_ref, left_ref, right_ref, v0, cell_buf, chigh, clow):
    zero5 = jnp.zeros((16, WIDE - TILE5), jnp.float32)

    def place(i, value):
        v0[16 * i:16 * i + 16, TILE5:] = zero5
        v0[16 * i:16 * i + 16, :OWN] = value

    own_lane = lax.broadcasted_iota(jnp.int32, (16, 128), 1) < SPLIT

    def ghost(i, ref, begin):
        v0[16 * i:16 * i + 16, :TILE5] = ref[:, begin:begin + TILE5]
        v0[16 * i:16 * i + 16, TILE5:] = jnp.where(own_lane, ref[:, begin + TILE5:begin + WIDE], 0.0)

    for i in range(3):
        ghost(i, left_ref, WIDE * i)
    for i in range(2):
        ghost(11 + i, right_ref, WIDE * i)
    v0[16 * 13:, :128] = right_ref[:, 2 * WIDE:]
    for i in range(8):
        place(3 + i, own_ref[:, i, :])
    cell_vectors(v0, 0, 13, cell_buf, chigh, clow)


def split_kernel(operator_ref, ksplit, kwide):
    kwide[720:, :] = jnp.zeros((WIDE - 720, WIDE), jnp.float32)
    kwide[:, TILE5:] = jnp.zeros((WIDE, WIDE - TILE5), jnp.float32)
    kwide[:NODES, :NODES] = operator_ref[...]
    for i in range(0, WIDE, 128):
        high, low = split2(kwide[i:i + 128, :])
        ksplit[i:i + 128, :] = high
        ksplit[WIDE + i:WIDE + i + 128, :] = low


def filter_kernel(last_ref, scale_ref, own_ref, left_ref, right_ref, part_ref, ksplit, out_ref,
                  v0, v1, v2, chigh, clow, cell_buf, product, pot):
    for half in range(2):
        rho = (part_ref[half] + part_ref[half + 2]) + (part_ref[half + 4] + part_ref[half + 6])
        value = jnp.where(
            rho > 0.0, -0.7386 * jnp.exp(jnp.log(jnp.where(rho > 0.0, rho, 1.0)) * (1.0 / 3.0)), 0.0)
        for t in range(3):
            begin = half * HALF + 128 * t
            pot[:KEPT, begin:begin + 128] = value[KEPT * t:KEPT * t + KEPT, :]
    lane = lax.broadcasted_iota(jnp.int32, (16, 128), 1)
    is_face = lane < FACE
    is_own5 = lane < SPLIT

    def scale_of(i):
        if i < 3:
            line = left_ref[:, WIDE * i + OWN:WIDE * i + OWN + 1]
        elif i < 11:
            line = scale_ref[i - 3]
        else:
            line = right_ref[:, WIDE * (i - 11) + OWN:WIDE * (i - 11) + OWN + 1]
        return line

    alive = last_ref[0].astype(jnp.float32)

    def assemble(begin, end, product, cells, combine):
        tail = None
        for i in range(begin, end):
            r = slice(16 * i, 16 * i + 16)
            scale = scale_of(i)
            parts = []
            for t in range(6):
                c = slice(128 * t, 128 * t + 128)
                parts.append(scale * product[r, c] + pot[i:i + 1, c] * cells[r, c])
            if tail is not None:
                add = jnp.where(is_face, pltpu.roll(tail, 128 - SPLIT, 1), 0.0)
                if i == 11:
                    add = add * alive
                parts[0] = parts[0] + add
                for t in range(6):
                    value = parts[t]
                    if t == 5:
                        value = jnp.where(is_own5, value, 0.0)
                    combine(i, t, value)
            tail = parts[5]

    def apply(source, begin, end, combine):
        cell_vectors(source, begin, end, cell_buf, chigh, clow)
        products(begin, end, product, chigh, clow, ksplit)
        assemble(begin, end, product, cell_buf, combine)

    def at(ref, i, t):
        return ref[16 * i:16 * i + 16, 128 * t:128 * t + 128]

    def first(i, t, value):
        v1[16 * i:16 * i + 16, 128 * t:128 * t + 128] = (value - CENTER * at(v0, i, t)) * (1.0 / HALF_WIDTH)

    def second(i, t, value):
        v2[16 * i:16 * i + 16, 128 * t:128 * t + 128] = (value - CENTER * at(v1, i, t)) * (2.0 / HALF_WIDTH) - at(v0, i, t)

    def third(i, t, value):
        result = (value - CENTER * at(v2, i, t)) * (2.0 / HALF_WIDTH) - at(v1, i, t)
        if t < 5:
            out_ref[i - 3, :, 128 * t:128 * t + 128] = result
        else:
            out_ref[i - 3, :, TILE5:OWN] = result[:, :SPLIT]

    first_vectors(own_ref, left_ref, right_ref, v0, cell_buf, chigh, clow)
    products(0, 13, product, chigh, clow, ksplit)
    assemble(0, 13, product, cell_buf, first)
    apply(v1, 1, 12, second)
    apply(v2, 2, 11, third)


def solve_kernel(total, gram_ref, flat_ref, out_ref, inverse_ref):
    shape = (8, 128)
    col = lax.broadcasted_iota(jnp.int32, shape, 1)
    row = lax.broadcasted_iota(jnp.int32, shape, 0)
    a = [gram_ref[8 * i:8 * i + 8, :] * (1.0 / total) for i in range(16)]
    w = [jnp.where(col == row + 8 * i, 1.0, 0.0) for i in range(16)]

    def columns(block, k):
        return [jnp.broadcast_to(block[:, 8 * k + j:8 * k + j + 1], shape) for j in range(8)]

    def line(block, i):
        return jnp.broadcast_to(block[i:i + 1, :], shape)

    for k in range(16):
        own = columns(a[k], k)
        s = [[line(own[j], i) for j in range(i + 1)] for i in range(8)]
        low = [[None] * 8 for _ in range(8)]
        inv = [None] * 8
        for j in range(8):
            inv[j] = 1.0 / s[j][j]
            for i in range(j + 1, 8):
                low[i][j] = s[i][j] * inv[j]
            for i in range(j + 1, 8):
                for m in range(j + 1, i + 1):
                    s[i][m] = s[i][m] - low[i][j] * s[m][j]
        n = [[None] * 8 for _ in range(8)]
        for i in range(8):
            for j in range(i):
                value = low[i][j]
                for m in range(j + 1, i):
                    value = value + low[i][m] * n[m][j]
                n[i][j] = -value

        def forward(block):
            lines = [line(block, i) for i in range(8)]
            result = []
            for i in range(8):
                value = lines[i]
                for j in range(i):
                    value = value + n[i][j] * lines[j]
                result.append(value)
            return result

        def backward(lines):
            scaled = [inv[i] * lines[i] for i in range(8)]
            result = []
            for j in range(8):
                value = scaled[j]
                for i in range(j + 1, 8):
                    value = value + n[i][j] * scaled[i]
                result.append(value)
            return result

        lines_w = forward(w[k])
        final = jnp.zeros(shape, jnp.float32)
        for i in range(8):
            final = jnp.where(row == i, lines_w[i] * lax.rsqrt(s[i][i]), final)
        inverse_ref[8 * k:8 * k + 8, :] = final
        if k < 15:
            za = backward(forward(a[k]))
            zw = backward(lines_w)
            for i in range(k + 1, 16):
                c = columns(a[i], k)
                for j in range(8):
                    a[i] = a[i] - c[j] * za[j]
                    w[i] = w[i] - c[j] * zw[j]
    inverse_high, inverse_low = split2(inverse_ref[...])
    for begin in range(0, OWN, 128):
        c = slice(begin, min(begin + 128, OWN))
        flat_high, flat_low = split2(jnp.transpose(flat_ref[:, c]))
        out_ref[c, :] = (dot_nt(flat_high, inverse_high) + dot_nt(flat_low, inverse_high)
                         + dot_nt(flat_high, inverse_low))


def body(orbitals, cell_operator, cell_scale, density, block_owner, block_cell):
    dom_count = lax.axis_size("dom")
    band_count = lax.axis_size("band")
    dom = lax.axis_index("dom")
    core = jnp.reshape(lax.axis_index("band") % 2, (1,)).astype(jnp.int32)
    alive = jnp.reshape((dom < dom_count - 1).astype(jnp.int32), (1,))
    smem = pl.BlockSpec(memory_space=pltpu.SMEM)
    vmem = pl.BlockSpec(memory_space=pltpu.VMEM)
    hbm = pl.BlockSpec(memory_space=pltpu.HBM)
    params = pltpu.CompilerParams(vmem_limit_bytes=16 << 20)
    roomy = pltpu.CompilerParams(vmem_limit_bytes=62 << 20)

    count = density.shape[0]
    pack_shape = jax.ShapeDtypeStruct((HALF + 8, count), jnp.float32)
    left_shape = jax.ShapeDtypeStruct((16, 3 * WIDE), jnp.float32)
    right_shape = jax.ShapeDtypeStruct((16, 2 * WIDE + 128), jnp.float32)
    own, send = pl.pallas_call(
        pack_kernel,
        out_shape=(pack_shape, pack_shape),
        in_specs=[smem] + [hbm] * 3,
        out_specs=(vmem,) * 2,
        scratch_shapes=[
            pltpu.VMEM((1, count), jnp.int32),
            pltpu.VMEM((1, count), jnp.int32),
            pltpu.VMEM((NODES, count), jnp.float32),
            pltpu.SemaphoreType.DMA((3,)),
        ],
        compiler_params=roomy,
        name="pack",
    )(core, block_owner.reshape(1, -1), block_cell.reshape(1, -1), density.T)
    other = lax.ppermute(send, "band", [(i, i ^ 1) for i in range(band_count)])
    own = pl.pallas_call(
        own_kernel,
        out_shape=jax.ShapeDtypeStruct((4 * SLAB, HALF), jnp.float32),
        in_specs=[vmem],
        out_specs=vmem,
        compiler_params=params,
        name="own_sums",
    )(own)
    delivered = pl.pallas_call(
        deliver_kernel,
        out_shape=jax.ShapeDtypeStruct((4 * SLAB, HALF), jnp.float32),
        in_specs=[vmem, vmem],
        out_specs=vmem,
        compiler_params=params,
        name="deliver",
    )(own, other)

    send_left, send_right = pl.pallas_call(
        ghost_kernel,
        out_shape=(left_shape, right_shape),
        in_specs=[vmem, vmem],
        out_specs=(vmem, vmem),
        compiler_params=params,
        name="ghosts",
    )(cell_scale.reshape(1, -1), orbitals)
    left = lax.ppermute(send_left, "dom", [(i, i + 1) for i in range(dom_count - 1)])
    right = lax.ppermute(send_right, "dom", [(i + 1, i) for i in range(dom_count - 1)])

    part = exchange(delivered.reshape(4, SLAB, HALF), "dom", X_GROUPS)
    windows = pl.pallas_call(
        window_kernel,
        out_shape=jax.ShapeDtypeStruct((16, PACKED, 128), jnp.float32),
        in_specs=[vmem],
        out_specs=vmem,
        scratch_shapes=[pltpu.VMEM((SLAB, HALF), jnp.float32)],
        compiler_params=params,
        name="windows",
    )(part)
    windows, left, right = lax.optimization_barrier((windows, left, right))
    part = exchange(windows, "dom", YZ_GROUPS)
    window = jnp.sum(part, 0)
    window, operator = lax.optimization_barrier((window, cell_operator))
    part = exchange(jnp.broadcast_to(window[None], (band_count, PACKED, 128)), "band")

    ksplit = pl.pallas_call(
        split_kernel,
        out_shape=jax.ShapeDtypeStruct((2 * WIDE, WIDE), jnp.bfloat16),
        in_specs=[vmem],
        out_specs=vmem,
        scratch_shapes=[pltpu.VMEM((WIDE, WIDE), jnp.float32)],
        compiler_params=params,
        name="split_operator",
    )(operator)
    filtered = pl.pallas_call(
        filter_kernel,
        out_shape=jax.ShapeDtypeStruct((8, 16, OWN), jnp.float32),
        in_specs=[smem] * 2 + [vmem] * 5,
        out_specs=vmem,
        scratch_shapes=[
            pltpu.VMEM((224, WIDE), jnp.float32),
            pltpu.VMEM((224, WIDE), jnp.float32),
            pltpu.VMEM((224, WIDE), jnp.float32),
            pltpu.VMEM((224, WIDE), jnp.bfloat16),
            pltpu.VMEM((224, WIDE), jnp.bfloat16),
            pltpu.VMEM((224, WIDE), jnp.float32),
            pltpu.VMEM((224, WIDE), jnp.float32),
            pltpu.VMEM((16, WIDE), jnp.float32),
        ],
        compiler_params=params,
        name="chebyshev",
    )(alive, cell_scale, orbitals, left, right, part, ksplit)

    flat = exchange(filtered, "band").reshape(128, OWN)
    both = ("dom", "band")
    total = OWN * dom_count * band_count
    gram = jnp.dot(flat, flat.T, precision=lax.Precision.HIGH)
    part = jnp.sum(exchange(gram.reshape(16, 8, 128), both, NEAR_GROUPS), 0)
    part = jnp.sum(exchange(jnp.broadcast_to(part[None], (32, 8, 128)), both, FAR_GROUPS), 0)
    gram = exchange(jnp.broadcast_to(part[None], (16, 8, 128)), both, NEAR_GROUPS).reshape(128, 128)
    basis = pl.pallas_call(
        functools.partial(solve_kernel, float(total)),
        out_shape=jax.ShapeDtypeStruct((OWN, 128), jnp.float32),
        in_specs=[vmem, vmem],
        out_specs=vmem,
        scratch_shapes=[pltpu.VMEM((128, 128), jnp.float32)],
        compiler_params=params,
        name="orthonormalize",
    )(gram, flat)
    return basis.T.reshape(128, 1, OWN)


def solution(mesh):
    return jax.shard_map(
        body,
        mesh=mesh,
        in_specs=(
            P("band", "dom", None),
            P(),
            P("dom"),
            P(("dom", "band"), None),
            P(("dom", "band"), None),
            P(("dom", "band")),
        ),
        out_specs=P(None, ("dom", "band"), None),
        check_vma=False,
    )
```
